512 devices in a mesh: len: 16 (over z, core), wid: 8 (over y), hgt: 4 (over x).
Axes of the slice: x: 4, y: 8, z: 8, core: 2. Of those that a mesh axis runs over, the one named last changes fastest.
Arguments:
- pressure_now: float32 [64, 512, 2048], P('hgt', 'wid', 'len')
- pressure_old: float32 [64, 512, 2048], P('hgt', 'wid', 'len')
- classes: int32 [64, 512, 2048], P('hgt', 'wid', 'len'), may hold values from 0 to 8, as said below
- admittance: float32 [8], replicated, may hold values from 0.05 to 1.5
- source_cells: int32 [4, 3], replicated, may hold values from 0 to 2047, as said below
- source_signal: float32 [16, 4], replicated, may hold values from -6 to 6
- receiver_cells: int32 [128, 3], replicated, may hold values from 0 to 2047, as said below
Outputs:
- pressure: float32 [64, 512, 2048], P('hgt', 'wid', 'len')
- traces: float32 [16, 128], replicated
The draws below stay inside these ranges and needn't reach their ends.
Inputs may be any that keep to these rules, and one draw needn't show every extreme that they name: 0 is air; 1 to 8 are wall classes; every cell on the grid's outer faces is a wall. `source_cells`: each row holds a cell's height, width and length coordinates, inside the grid. `receiver_cells`: each row holds a cell's height, width and length coordinates, inside the grid.
All inputs are finite; a program needn't handle non-finite values.
Results may differ from the reference program's by a relative error of at most 0.000022.
Values sent between devices are 32-bit elements; how exact they have to be, the bound alone decides.
No kernel may reach another device: no remote copies, remote signals or barrier semaphores. Data moves between devices by JAX's collectives and lax.ppermute only.
A program may use at most 64 MiB of HBM per device.

```python
import math
import jax
import jax.numpy as jnp

STEPS = 16
NSRC = 4
NREC = 128
NCLASS = 8
NH = 64
NW = 512
NL = 2048


def field_draw(key):
    shape = (NH, NW, NL)
    return jax.random.normal(key, shape, jnp.float32)


def draw_pressure_now(key, part):
    key = jax.random.fold_in(key, 11)
    return field_draw(key)


def draw_pressure_old(key, part):
    key = jax.random.fold_in(key, 12)
    return field_draw(key)


def draw_classes(key, part):
    key = jax.random.fold_in(key, 13)
    first, second = jax.random.split(key, 2)
    shape = (NH, NW, NL)
    wall_kind = jax.random.randint(first, shape, 1, NCLASS + 1)
    obstacle = jax.random.randint(second, shape, 0, 8) == 0
    rows = jnp.arange(NH)[:, None, None]
    cols = jnp.arange(NW)[None, :, None]
    deep = jnp.arange(NL)[None, None, :]
    face = (rows == 0) | (rows == NH - 1) | (cols == 0) | (cols == NW - 1) | (deep == 0) | (deep == NL - 1)
    return jnp.where(face | obstacle, wall_kind, 0).astype(jnp.int32)


def coordinates(key, count):
    first, second, third = jax.random.split(key, 3)
    rows = jax.random.randint(first, (count,), 0, NH)
    cols = jax.random.randint(second, (count,), 0, NW)
    deep = jax.random.randint(third, (count,), 0, NL)
    deep = deep.at[0].set(NL - 1)
    deep = deep.at[1].set(0)
    return jnp.stack([rows, cols, deep], axis=1).astype(jnp.int32)


def draw_source_cells(key, part):
    key = jax.random.fold_in(key, 14)
    return coordinates(key, NSRC)


def draw_receiver_cells(key, part):
    key = jax.random.fold_in(key, 15)
    return coordinates(key, NREC)


def bell_draw(key, extent, spread, most, kind=jnp.bfloat16):
    return jnp.clip(spread * jax.random.normal(key, extent, jnp.float32), -most, most).astype(kind)


def setup_inputs(seed: int = 0) -> dict:
    key_of = jax.random.split(jax.random.key(seed), 8)
    pressure_now = draw_pressure_now(jax.random.fold_in(key_of[7], 71), 0)
    pressure_old = draw_pressure_old(jax.random.fold_in(key_of[7], 71), 0)
    classes = draw_classes(jax.random.fold_in(key_of[7], 71), 0)
    admittance = jnp.clip(jnp.exp(jax.random.uniform(key_of[3], (NCLASS,), jnp.float32, math.log(0.05), math.log(1.5))), 0.05, 1.5)
    source_cells = draw_source_cells(jax.random.fold_in(key_of[7], 71), 0)
    source_signal = bell_draw(key_of[5], (STEPS, NSRC), 1.0, 6.0, jnp.float32)
    receiver_cells = draw_receiver_cells(jax.random.fold_in(key_of[7], 71), 0)
    return {"pressure_now": pressure_now, "pressure_old": pressure_old, "classes": classes, "admittance": admittance, "source_cells": source_cells, "source_signal": source_signal, "receiver_cells": receiver_cells}


courant_sq = 1.0 / 3.0


def lookup(classes, admittance):
    loss = jnp.zeros(classes.shape, jnp.float32)
    for index in range(admittance.shape[0]):
        loss = loss + jnp.where(classes == index + 1, admittance[index], jnp.float32(0.0))
    return loss


def update(now, old, padded, loss):
    beside = padded[2:, 1:-1, 1:-1] + padded[:-2, 1:-1, 1:-1]
    beside = beside + padded[1:-1, 2:, 1:-1] + padded[1:-1, :-2, 1:-1]
    beside = beside + padded[1:-1, 1:-1, 2:] + padded[1:-1, 1:-1, :-2]
    return (2.0 * now - (1.0 - loss) * old + courant_sq * (beside - 6.0 * now)) / (1.0 + loss)


def reference(pressure_now, pressure_old, classes, admittance, source_cells, source_signal, receiver_cells):
    loss = lookup(classes, admittance)
    now, old = pressure_now, pressure_old
    traces = []
    for step in range(STEPS):
        fresh = update(now, old, jnp.pad(now, 1), loss)
        fresh = fresh.at[source_cells[:, 0], source_cells[:, 1], source_cells[:, 2]].add(source_signal[step])
        old, now = now, fresh
        traces.append(now[receiver_cells[:, 0], receiver_cells[:, 1], receiver_cells[:, 2]])
    return now, jnp.stack(traces)
```

```python
import functools

import jax
import jax.numpy as jnp
from jax import lax
from jax.experimental import pallas as pl
from jax.experimental.pallas import tpu as pltpu
from jax.sharding import PartitionSpec as P

STEPS = 16
HALO = 16
LANES = 128
HIGH, WIDE, DEEP = 16, 64, 128
TALL = HIGH + 2 * HALO
BROAD = WIDE + 2 * HALO
COLS = BROAD // 8
CHUNK = 4
VMEM = pl.BlockSpec(memory_space=pltpu.VMEM)
SMEM = pl.BlockSpec(memory_space=pltpu.SMEM)


def lane_ids():
    return lax.broadcasted_iota(jnp.int32, (8, LANES), 1)


def regroup(rows, order):
    return jnp.take_along_axis(rows, order, axis=1, mode="promise_in_bounds")


def even_odd():
    lane = lane_ids()
    return jnp.where(lane < 64, 2 * lane, 2 * lane - 127)


def in_order():
    lane = lane_ids()
    return (lane // 2) + 64 * (lane % 2)


def pack_kernel(adm_ref, now_ref, old_ref, cls_ref, s_ref, left_ref, right_ref):
    lane = lane_ids()
    order = even_odd()

    def layer(h, carry):
        heads, tails = [], []
        for j in range(WIDE // 8):
            rows = pl.ds(8 * j, 8)
            kinds = cls_ref[h, rows, :]
            loss = jnp.zeros((8, LANES), jnp.float32)
            for index in range(adm_ref.shape[0]):
                loss = loss + jnp.where(kinds == index + 1, adm_ref[index], jnp.float32(0.0))
            gain = jnp.float32(1.0 / 3.0) / (1.0 + loss)
            head = jnp.zeros((8, LANES), jnp.float32)
            tail = jnp.zeros((8, LANES), jnp.float32)
            for a, field in enumerate((now_ref[h, rows, :], old_ref[h, rows, :], gain)):
                split = regroup(field, order)
                s_ref[a, h, rows, :] = split
                for parity in range(2):
                    at = 8 * (2 * a + parity)
                    inside = (lane >= at) & (lane < at + 8)
                    head = jnp.where(inside, pltpu.roll(split, (at - 64 * parity) % LANES, 1), head)
                    tail = jnp.where(
                        inside, pltpu.roll(split, (at - 56 - 64 * parity) % LANES, 1), tail
                    )
            heads.append(head)
            tails.append(tail)
        half = WIDE // 16
        for j in range(half):
            rows = pl.ds(8 * j, 8)
            left_ref[h, rows, :] = heads[j] + pltpu.roll(heads[j + half], 64, 1)
            right_ref[h, rows, :] = tails[j] + pltpu.roll(tails[j + half], 64, 1)
        return carry

    lax.fori_loop(0, HIGH, layer, 0)


def edge_kernel(from_right_ref, from_left_ref, e_ref):
    lane = lane_ids()

    def layer(h, carry):
        half = WIDE // 16
        for j in range(half):
            rows = pl.ds(8 * j, 8)
            a, b = from_right_ref[h, rows, :], from_left_ref[h, rows, :]
            first = jnp.where(lane < 48, a, jnp.float32(0.0))
            first = jnp.where((lane >= 56) & (lane < 104), pltpu.roll(b, 56, 1), first)
            second = jnp.where(lane < 48, pltpu.roll(a, 64, 1), jnp.float32(0.0))
            second = jnp.where((lane >= 56) & (lane < 104), pltpu.roll(b, 120, 1), second)
            e_ref[h, rows, :] = first
            e_ref[h, pl.ds(8 * (j + half), 8), :] = second
        return carry

    lax.fori_loop(0, HIGH, layer, 0)


def march_kernel(
    src_ref, sig_ref, rec_ref, *refs
):
    pieces = refs[:18]
    out_ref, trace_ref = refs[18:20]
    a_ref, b_ref, p_ref, temp, plain, hist, todo = refs[20:]
    lane = lane_ids()
    row = lax.broadcasted_iota(jnp.int32, (8, LANES), 0)
    zero = jnp.float32(0.0)
    fringe = ((lane >= 64) & (lane < 72)) | (lane >= 120)
    corner = (
        lax.axis_index("hgt") * HIGH - HALO,
        lax.axis_index("wid") * WIDE - HALO,
        lax.axis_index("len") * DEEP,
    )

    for part in range(3):
        cells = pieces[6 * part : 6 * part + 3]
        edges = pieces[6 * part + 3 : 6 * part + 6]

        def layer(h, carry):
            at = part * HIGH + h
            for k, (lo, n) in enumerate(((0, 16), (16, 64), (80, 16))):
                for a in range(3):
                    temp[a, pl.ds(lo, n), :] = cells[k][a, h]
                temp[3, pl.ds(lo, n), :] = edges[k][h]
            for j in range(COLS):
                edge = temp[3, pl.ds(j, 8, stride=COLS), :]
                for a, ref in enumerate((a_ref, b_ref, p_ref)):
                    main = temp[a, pl.ds(j, 8, stride=COLS), :]
                    for parity in range(2):
                        near = pltpu.roll(edge, 64 - 8 * (2 * a + parity), 1)
                        near = jnp.where(fringe, near, zero)
                        mid = pltpu.roll(main, 64, 1) if parity else main
                        ref[parity, at, j] = jnp.where(lane < 64, mid, near)
            return carry

        lax.fori_loop(0, HIGH, layer, 0)

    def note(r, count):
        h = rec_ref[0, r] - corner[0]
        w = rec_ref[1, r] - corner[1]
        d = rec_ref[2, r] - corner[2]
        mine = (h >= HALO) & (h < HALO + HIGH) & (w >= HALO) & (w < HALO + WIDE)
        mine = mine & (d >= 0) & (d < DEEP)

        @pl.when(mine)
        def _():
            todo[0, count] = r
            todo[1, count] = h
            todo[2, count] = w % COLS
            todo[3, count] = w // COLS
            todo[4, count] = d % 2
            todo[5, count] = d // 2

        return count + mine.astype(jnp.int32)

    count = lax.fori_loop(0, rec_ref.shape[1], note, jnp.int32(0))

    points = []
    for s in range(src_ref.shape[0]):
        h = src_ref[s, 0] - corner[0]
        w = src_ref[s, 1] - corner[1]
        d = src_ref[s, 2] - corner[2] + HALO
        near = (h >= 0) & (h < TALL) & (w >= 0) & (w < BROAD) & (d >= 0) & (d < DEEP + 2 * HALO)
        h = jnp.clip(h, 0, TALL - 1)
        w = jnp.clip(w, 0, BROAD - 1)
        d = jnp.clip(d, 0, DEEP + 2 * HALO - 1)
        place = (d // 2 + LANES - HALO // 2) % LANES
        points.append((near, d % 2, h, w % COLS, (row == w // COLS) & (lane == place)))

    def step(now, old, t):
        def chunk(i, carry):
            for u in range(CHUNK):
                h = t + 1 + CHUNK * i + u
                for parity in range(2):
                    other = [now[1 - parity, h, j] for j in range(COLS)]
                    mine = [now[parity, h, j] for j in range(COLS)]
                    for j in range(COLS):
                        before = mine[j - 1] if j > 0 else pltpu.roll(mine[COLS - 1], 1, 0)
                        after = mine[j + 1] if j < COLS - 1 else pltpu.roll(mine[0], 7, 0)
                        beside = other[j] + pltpu.roll(other[j], 127 if parity else 1, 1)
                        total = (now[parity, h - 1, j] + now[parity, h + 1, j]) + (before + after)
                        total = total + beside
                        past = old[parity, h, j]
                        old[parity, h, j] = past + p_ref[parity, h, j] * (total - 6.0 * past)
            return carry

        trips = (TALL - 2 * (t + 1) + CHUNK - 1) // CHUNK
        lax.fori_loop(0, trips, chunk, 0)
        for s, (near, parity, h, j, spot) in enumerate(points):

            @pl.when(near)
            def _():
                old[parity, h, j] = old[parity, h, j] + jnp.where(spot, sig_ref[t, s], zero)

        def keep(i, carry):
            value = old[todo[4, i], todo[1, i], todo[2, i], pl.ds(todo[3, i], 1), :]
            hist[i, pl.ds(t, 1), :] = value
            return carry

        lax.fori_loop(0, count, keep, 0)

    def pair(i, carry):
        step(a_ref, b_ref, 2 * i)
        step(b_ref, a_ref, 2 * i + 1)
        return carry

    lax.fori_loop(0, STEPS // 2, pair, 0)

    trace_ref[...] = jnp.zeros((STEPS, LANES), jnp.float32)
    wide_lane = lax.broadcasted_iota(jnp.int32, (STEPS, LANES), 1)

    def gather(i, carry):
        number = todo[0, i]
        moved = pltpu.roll(hist[i], (number - todo[5, i] + LANES) % LANES, 1)
        trace_ref[...] = jnp.where(wide_lane == number, moved, trace_ref[...])
        return carry

    lax.fori_loop(0, count, gather, 0)

    order = in_order()

    def finish(h, carry):
        for j in range(COLS):
            even, odd = a_ref[0, HALO + h, j], a_ref[1, HALO + h, j]
            joined = jnp.where(lane < 64, even, pltpu.roll(odd, 64, 1))
            plain[pl.ds(j, 8, stride=COLS), :] = regroup(joined, order)
        out_ref[h] = plain[pl.ds(HALO, WIDE), :]
        return carry

    lax.fori_loop(0, HIGH, finish, 0)


def field(*shape):
    return jax.ShapeDtypeStruct(shape, jnp.float32)


def pack(admittance, now, old, classes):
    return pl.pallas_call(
        pack_kernel,
        out_shape=(
            field(3, HIGH, WIDE, LANES),
            field(HIGH, WIDE // 2, LANES),
            field(HIGH, WIDE // 2, LANES),
        ),
        in_specs=[SMEM, VMEM, VMEM, VMEM],
        out_specs=(VMEM, VMEM, VMEM),
        name="pack",
        compiler_params=pltpu.CompilerParams(vmem_limit_bytes=12 << 20),
    )(admittance, now, old, classes)


def edge(from_right, from_left):
    return pl.pallas_call(
        edge_kernel,
        out_shape=field(HIGH, WIDE, LANES),
        in_specs=[VMEM, VMEM],
        out_specs=VMEM,
        name="edge",
        compiler_params=pltpu.CompilerParams(vmem_limit_bytes=12 << 20),
    )(from_right, from_left)


def march(sources, signal, receivers, pieces):
    return pl.pallas_call(
        march_kernel,
        out_shape=(field(HIGH, WIDE, DEEP), field(STEPS, LANES)),
        in_specs=[SMEM] * 3 + [VMEM] * 18,
        out_specs=(VMEM, VMEM),
        scratch_shapes=[
            pltpu.VMEM((2, TALL + 4, COLS, 8, LANES), jnp.float32),
            pltpu.VMEM((2, TALL + 4, COLS, 8, LANES), jnp.float32),
            pltpu.VMEM((2, TALL + 4, COLS, 8, LANES), jnp.float32),
            pltpu.VMEM((4, BROAD, LANES), jnp.float32),
            pltpu.VMEM((BROAD, LANES), jnp.float32),
            pltpu.VMEM((LANES, STEPS, LANES), jnp.float32),
            pltpu.SMEM((8, LANES), jnp.int32),
        ],
        name="march",
        compiler_params=pltpu.CompilerParams(vmem_limit_bytes=52 << 20),
    )(sources, signal, receivers, *pieces)


def shift(x, axes, moves):
    sizes = [lax.axis_size(a) for a in axes]
    pairs = []
    for start in range(functools.reduce(lambda a, b: a * b, sizes)):
        place, rest = [], start
        for size in reversed(sizes):
            place.insert(0, rest % size)
            rest //= size
        goal = [a + b for a, b in zip(place, moves)]
        if all(0 <= g < size for g, size in zip(goal, sizes)):
            end = 0
            for g, size in zip(goal, sizes):
                end = end * size + g
            pairs.append((start, end))
    return lax.ppermute(x, axes if len(axes) > 1 else axes[0], pairs)


def spread(x):
    rows = x.ndim - 2
    head = lax.slice_in_dim(x, 0, HALO, axis=rows)
    tail = lax.slice_in_dim(x, WIDE - HALO, WIDE, axis=rows)
    both = ("wid", "hgt")
    return [
        [shift(tail, both, (1, 1)), shift(x, ("hgt",), (1,)), shift(head, both, (-1, 1))],
        [shift(tail, ("wid",), (1,)), x, shift(head, ("wid",), (-1,))],
        [shift(tail, both, (1, -1)), shift(x, ("hgt",), (-1,)), shift(head, both, (-1, -1))],
    ]


def report(values):
    count = lax.axis_size("len")
    pairs = [[2 * i, 2 * i + 1] for i in range(count // 2)]
    column = [list(range(core, count, 2)) for core in range(2)]
    values = lax.psum(values, "len", axis_index_groups=pairs)

    def total(values, axes, size, groups=None):
        copies = jnp.broadcast_to(values[None], (size,) + values.shape)
        got = lax.all_to_all(copies, axes, 0, 0, axis_index_groups=groups, tiled=True)
        return jnp.sum(got, axis=0)

    values = total(values, "len", count // 2, column)
    sides = lax.axis_size("wid") * lax.axis_size("hgt")
    return total(values, ("wid", "hgt"), sides)


def per_device(
    pressure_now, pressure_old, classes, admittance, source_cells, source_signal, receiver_cells
):
    s, to_left, to_right = pack(admittance, pressure_now, pressure_old, classes)
    from_right = shift(to_left, ("len",), (-1,))
    from_left = shift(to_right, ("len",), (1,))
    cells = spread(s)
    edges = spread(edge(from_right, from_left))
    pieces = []
    for part in range(3):
        pieces += cells[part] + edges[part]
    now, traces = march(source_cells, source_signal, receiver_cells.T, pieces)
    return now, report(traces)


def solution(mesh):
    block = P("hgt", "wid", "len")
    return jax.shard_map(
        per_device,
        mesh=mesh,
        in_specs=(block, block, block, P(), P(), P(), P()),
        out_specs=(block, P()),
        check_vma=False,
    )
```

```python
import functools

import jax
import jax.numpy as jnp
from jax import lax
from jax.experimental import pallas as pl
from jax.experimental.pallas import tpu as pltpu
from jax.sharding import PartitionSpec as P

STEPS = 16
HALO = 16
LANES = 128
HIGH, WIDE, DEEP = 16, 64, 128
HALF = HIGH // 2
TALL = HIGH + 2 * HALO
BROAD = WIDE + 2 * HALO
COLS = BROAD // 8
RIM = 3 * 2 * HALO + BROAD
VMEM = pl.BlockSpec(memory_space=pltpu.VMEM)
SMEM = pl.BlockSpec(memory_space=pltpu.SMEM)


def lane_ids():
    return lax.broadcasted_iota(jnp.int32, (8, LANES), 1)


def regroup(rows, order):
    return jnp.take_along_axis(rows, order, axis=1, mode="promise_in_bounds")


def even_odd():
    lane = lane_ids()
    return jnp.where(lane < 64, 2 * lane, 2 * lane - 127)


def in_order():
    lane = lane_ids()
    return (lane // 2) + 64 * (lane % 2)


def pack_kernel(adm_ref, now_ref, old_ref, cls_ref, s_ref, left_ref, right_ref):
    lane = lane_ids()
    order = even_odd()

    def layer(h, carry):
        rims = []
        for j in range(WIDE // 8):
            rows = pl.ds(8 * j, 8)
            kinds = cls_ref[h, rows, :]
            loss = jnp.zeros((8, LANES), jnp.float32)
            for index in range(adm_ref.shape[0]):
                loss = jnp.where(kinds == index + 1, adm_ref[index], loss)
            gain = jnp.float32(1.0 / 3.0) / (1.0 + loss)
            rim = None
            for a, field in enumerate((now_ref[h, rows, :], old_ref[h, rows, :], gain)):
                split = regroup(field, order)
                s_ref[h, a, rows, :] = split
                moved = pltpu.roll(split, 72, 1)
                both = jnp.where((lane < 8) | ((lane >= 56) & (lane < 64)), split, moved)
                if a == 0:
                    rim = both
                else:
                    both = pltpu.roll(both, 16 * a, 1)
                    here = (lane >= 16 * a) & (lane < 16 * a + 16)
                    here = here | ((lane >= 56 + 16 * a) & (lane < 72 + 16 * a))
                    rim = jnp.where(here, both, rim)
            rims.append(rim)
        half = WIDE // 16
        for j in range(half):
            rows = pl.ds(8 * j, 8)
            other = pltpu.roll(rims[j + half], 64, 1)
            left_ref[h, rows, :] = jnp.where(lane < 56, rims[j], other)
            right_ref[h, rows, :] = jnp.where((lane >= 56) & (lane < 104), rims[j], other)
        return carry

    lax.fori_loop(0, now_ref.shape[0], layer, 0)


def edge_kernel(from_right_ref, from_left_ref, s_ref, e_ref, head_ref, tail_ref):
    lane = lane_ids()
    zero = jnp.float32(0.0)
    used = (lane < 48) | ((lane >= 56) & (lane < 104))

    def layer(h, carry):
        half = WIDE // 16
        for j in range(half):
            rows = pl.ds(8 * j, 8)
            a, b = from_right_ref[h, rows, :], from_left_ref[h, rows, :]
            first = jnp.where(lane < 48, a, b)
            second = pltpu.roll(jnp.where((lane >= 64) & (lane < 112), a, b), 64, 1)
            e_ref[h, rows, :] = jnp.where(used, first, zero)
            e_ref[h, pl.ds(8 * (j + half), 8), :] = jnp.where(used, second, zero)
        for a in range(3):
            head_ref[h, a] = s_ref[h, a, pl.ds(0, HALO), :]
            tail_ref[h, a] = s_ref[h, a, pl.ds(WIDE - HALO, HALO), :]
        head_ref[h, 3] = e_ref[h, pl.ds(0, HALO), :]
        tail_ref[h, 3] = e_ref[h, pl.ds(WIDE - HALO, HALO), :]
        return carry

    lax.fori_loop(0, HIGH, layer, 0)


def beside_lanes(i):
    lane = lane_ids()
    k = lane % 8
    n = (HALO - i) // 2
    right = lane < 48
    return right, n, (right & (k < n)) | (~right & (k >= 8 - n))


def rim_kernel(e_ref, before_ref, after_ref, low_ref, top_ref):
    row = lax.broadcasted_iota(jnp.int32, (HALO, LANES), 0)

    def pair(out_ref, i, near, far):
        for a in range(3):
            at = 2 * HALO * a
            kept = jnp.where(row > i, before_ref[near, a], pltpu.roll(before_ref[far, a], i, 0))
            out_ref[i, pl.ds(at, HALO), :] = kept
            moved = pltpu.roll(after_ref[far, a], (HALO - i) % HALO, 0)
            out_ref[i, pl.ds(at + HALO, HALO), :] = jnp.where(row < HALO - i - 1, after_ref[near, a], moved)
        right, n, mask = beside_lanes(i)
        for j in range(COLS):
            if j < HALO // 8:
                a, b = before_ref[near, 3, pl.ds(8 * j, 8), :], before_ref[far, 3, pl.ds(8 * j, 8), :]
            elif j < COLS - HALO // 8:
                at = 8 * j - HALO
                a, b = e_ref[near, pl.ds(at, 8), :], e_ref[far, pl.ds(at, 8), :]
            else:
                at = 8 * j - HALO - WIDE
                a, b = after_ref[near, 3, pl.ds(at, 8), :], after_ref[far, 3, pl.ds(at, 8), :]
            moved = jnp.where(right, pltpu.roll(b, n, 1), pltpu.roll(b, LANES - n, 1))
            out_ref[i, pl.ds(6 * HALO + 8 * j, 8), :] = jnp.where(mask, a, moved)

    def both(i, carry):
        pair(low_ref, i, i, HIGH - 1 - i)
        pair(top_ref, i, HIGH - 1 - i, i)
        return carry

    lax.fori_loop(0, HALF, both, 0)


def fill(refs, temp, at):
    lane = lane_ids()
    zero = jnp.float32(0.0)
    fringe = ((lane >= 64) & (lane < 72)) | (lane >= 120)
    for j in range(COLS):
        edge = temp[3, pl.ds(j, 8, stride=COLS), :]
        for a, ref in enumerate(refs):
            main = temp[a, pl.ds(j, 8, stride=COLS), :]
            for parity in range(2):
                near = pltpu.roll(edge, 64 - 8 * (2 * a + parity), 1)
                near = jnp.where(fringe, near, zero)
                mid = pltpu.roll(main, 64, 1) if parity else main
                ref[parity, at, j] = jnp.where(lane < 64, mid, near)


def fill_own(refs, temp, s_ref, e_ref, before_ref, after_ref):
    def layer(h, carry):
        for a in range(3):
            temp[a, pl.ds(HALO, WIDE), :] = s_ref[h, a]
        temp[3, pl.ds(HALO, WIDE), :] = e_ref[h]
        for a in range(4):
            temp[a, pl.ds(0, HALO), :] = before_ref[h, a]
            temp[a, pl.ds(HALO + WIDE, HALO), :] = after_ref[h, a]
        fill(refs, temp, HALO + h)
        return carry

    lax.fori_loop(0, HIGH, layer, 0)


def fill_beside(refs, temp, s_ref, rim_ref, layers):
    def pair(i, carry):
        near, far = layers(i)
        for a in range(3):
            temp[a, pl.ds(0, HALO), :] = rim_ref[i, pl.ds(2 * HALO * a, HALO), :]
            temp[a, pl.ds(HALO, WIDE), :] = s_ref[near % HIGH, a]
            temp[a, pl.ds(HALO + WIDE, HALO), :] = rim_ref[i, pl.ds(2 * HALO * a + HALO, HALO), :]
        temp[3] = rim_ref[i, pl.ds(6 * HALO, BROAD), :]
        fill(refs, temp, near)
        for a in range(3):
            before = rim_ref[i, pl.ds(2 * HALO * a, HALO), :]
            temp[a, pl.ds(0, HALO), :] = pltpu.roll(before, (HALO - i) % HALO, 0)
            temp[a, pl.ds(HALO, WIDE), :] = s_ref[far % HIGH, a]
            after = rim_ref[i, pl.ds(2 * HALO * a + HALO, HALO), :]
            temp[a, pl.ds(HALO + WIDE, HALO), :] = pltpu.roll(after, i, 0)
        right, n, _ = beside_lanes(i)
        k = lane_ids() % 8
        mask = (right & (k < 8 - n)) | (~right & (k >= n))
        for j in range(COLS):
            both = rim_ref[i, pl.ds(6 * HALO + 8 * j, 8), :]
            moved = jnp.where(right, pltpu.roll(both, LANES - n, 1), pltpu.roll(both, n, 1))
            temp[3, pl.ds(8 * j, 8), :] = jnp.where(mask, moved, jnp.float32(0.0))
        fill(refs, temp, far)
        return carry

    lax.fori_loop(0, HALF, pair, 0)


def corner():
    return (
        lax.axis_index("hgt") * HIGH - HALO,
        lax.axis_index("wid") * WIDE - HALO,
        lax.axis_index("len") * DEEP,
    )


def list_receivers(rec_ref, todo):
    start = corner()

    def note(r, count):
        h = rec_ref[0, r] - start[0]
        w = rec_ref[1, r] - start[1]
        d = rec_ref[2, r] - start[2]
        mine = (h >= HALO) & (h < HALO + HIGH) & (w >= HALO) & (w < HALO + WIDE)
        mine = mine & (d >= 0) & (d < DEEP)

        @pl.when(mine)
        def _():
            todo[0, count] = r
            todo[1, count] = h
            todo[2, count] = w % COLS
            todo[3, count] = w // COLS
            todo[4, count] = d % 2
            todo[5, count] = d // 2

        return count + mine.astype(jnp.int32)

    return lax.fori_loop(0, rec_ref.shape[1], note, jnp.int32(0))


def list_sources(src_ref):
    lane = lane_ids()
    row = lax.broadcasted_iota(jnp.int32, (8, LANES), 0)
    start = corner()
    points = []
    for s in range(src_ref.shape[0]):
        h = src_ref[s, 0] - start[0]
        w = src_ref[s, 1] - start[1]
        d = src_ref[s, 2] - start[2] + HALO
        near = (h >= 0) & (h < TALL) & (w >= 0) & (w < BROAD) & (d >= 0) & (d < DEEP + 2 * HALO)
        h = jnp.clip(h, 0, TALL - 1)
        w = jnp.clip(w, 0, BROAD - 1)
        d = jnp.clip(d, 0, DEEP + 2 * HALO - 1)
        place = (d // 2 + LANES - HALO // 2) % LANES
        points.append((near, d % 2, h, w % COLS, (row == w // COLS) & (lane == place)))
    return points


def sweep(now, old, p_ref, low, high):
    def chunk(first, layers):
        for u in range(layers):
            h = first + u
            for parity in range(2):
                other = [now[1 - parity, h, j] for j in range(COLS)]
                mine = [now[parity, h, j] for j in range(COLS)]
                for j in range(COLS):
                    before = mine[j - 1] if j > 0 else pltpu.roll(mine[COLS - 1], 1, 0)
                    after = mine[j + 1] if j < COLS - 1 else pltpu.roll(mine[0], 7, 0)
                    beside = other[j] + pltpu.roll(other[j], 127 if parity else 1, 1)
                    total = (now[parity, h - 1, j] + now[parity, h + 1, j]) + (before + after)
                    total = total + beside
                    past = old[parity, h, j]
                    old[parity, h, j] = past + p_ref[parity, h, j] * (total - 6.0 * past)

    fours = (high - low) // 4

    def four(i, carry):
        chunk(low + 4 * i, 4)
        return carry

    def two(i, carry):
        chunk(low + 4 * fours + 2 * i, 2)
        return carry

    lax.fori_loop(0, fours, four, 0)
    lax.fori_loop(0, (high - low - 4 * fours) // 2, two, 0)


def march_kernel(src_ref, sig_ref, rec_ref, *refs):
    s_ref, e_ref, before_ref, after_ref = refs[:4]
    under, under_rim, over, over_rim = refs[4:8]
    out_ref, trace_ref = refs[8:10]
    a_ref, b_ref, p_ref, temp, hist, todo = refs[10:]
    zero = jnp.float32(0.0)
    fields = (a_ref, b_ref, p_ref)

    fill_own(fields, temp, s_ref, e_ref, before_ref, after_ref)
    fill_beside(fields, temp, under, under_rim, lambda i: (HALO - 1 - i, i))
    fill_beside(fields, temp, over, over_rim, lambda i: (HALO + HIGH + i, TALL - 1 - i))

    count = list_receivers(rec_ref, todo)
    points = list_sources(src_ref)

    def step(now, old, t):
        sweep(now, old, p_ref, t + 1, TALL - t - 1)
        for s, (near, parity, h, j, spot) in enumerate(points):

            @pl.when(near)
            def _():
                old[parity, h, j] = old[parity, h, j] + jnp.where(spot, sig_ref[t, s], zero)

        def keep(i, carry):
            value = old[todo[4, i], todo[1, i], todo[2, i], pl.ds(todo[3, i], 1), :]
            hist[i, pl.ds(t, 1), :] = value
            return carry

        lax.fori_loop(0, count, keep, 0)

    def pair(i, carry):
        step(a_ref, b_ref, 2 * i)
        step(b_ref, a_ref, 2 * i + 1)
        return carry

    lax.fori_loop(0, STEPS // 2, pair, 0)

    trace_ref[0] = jnp.zeros((STEPS, LANES), jnp.float32)
    wide_lane = lax.broadcasted_iota(jnp.int32, (STEPS, LANES), 1)

    def gather(i, carry):
        number = todo[0, i]
        moved = pltpu.roll(hist[i], (number - todo[5, i] + LANES) % LANES, 1)
        trace_ref[0] = jnp.where(wide_lane == number, moved, trace_ref[0])
        return carry

    lax.fori_loop(0, count, gather, 0)
    for i in range(1, trace_ref.shape[0]):
        trace_ref[i] = trace_ref[0]

    lane = lane_ids()
    plain = temp.at[0]

    def hand_on(h, carry):
        for j in range(COLS):
            even, odd = a_ref[0, HALO + h, j], a_ref[1, HALO + h, j]
            joined = jnp.where(lane < 64, even, pltpu.roll(odd, 64, 1))
            plain[pl.ds(j, 8, stride=COLS), :] = joined
        out_ref[h] = plain[pl.ds(HALO, WIDE), :]
        return carry

    lax.fori_loop(0, HIGH, hand_on, 0)


def order_kernel(split_ref, out_ref):
    order = in_order()

    def layer(h, carry):
        for j in range(WIDE // 8):
            rows = pl.ds(8 * j, 8)
            out_ref[h, rows, :] = regroup(split_ref[h, rows, :], order)
        return carry

    lax.fori_loop(0, split_ref.shape[0], layer, 0)


def relay_kernel(got_ref, out_ref):
    total = got_ref[0]
    for i in range(1, got_ref.shape[0]):
        total = total + got_ref[i]
    for i in range(out_ref.shape[0]):
        out_ref[i] = total


def field(*shape):
    return jax.ShapeDtypeStruct(shape, jnp.float32)


def call(kernel, name, outs, ins, scratch=(), scalars=0, limit=8):
    return pl.pallas_call(
        kernel,
        out_shape=tuple(field(*shape) for shape in outs),
        in_specs=[SMEM] * scalars + [VMEM] * (len(ins) - scalars),
        out_specs=tuple(VMEM for _ in outs),
        scratch_shapes=list(scratch),
        name=name,
        compiler_params=pltpu.CompilerParams(vmem_limit_bytes=limit << 20),
    )(*ins)


def shift(x, axis, move):
    size = lax.axis_size(axis)
    pairs = [(i, i + move) for i in range(size) if 0 <= i + move < size]
    return lax.ppermute(x, axis, pairs)


def per_device(
    pressure_now, pressure_old, classes, admittance, source_cells, source_signal, receiver_cells
):
    parts = 4
    layers = HIGH // parts

    def block(*shape):
        return pl.BlockSpec((layers,) + shape, lambda i: (i,) + (0,) * len(shape))

    s, to_left, to_right = pl.pallas_call(
        pack_kernel,
        grid=(parts,),
        out_shape=(
            field(HIGH, 3, WIDE, LANES),
            field(HIGH, WIDE // 2, LANES),
            field(HIGH, WIDE // 2, LANES),
        ),
        in_specs=[SMEM] + [block(WIDE, LANES)] * 3,
        out_specs=(block(3, WIDE, LANES), block(WIDE // 2, LANES), block(WIDE // 2, LANES)),
        name="pack",
        compiler_params=pltpu.CompilerParams(vmem_limit_bytes=8 << 20),
    )(admittance, pressure_now, pressure_old, classes)
    from_right = shift(to_left, "len", -1)
    from_left = shift(to_right, "len", 1)
    over, under = shift(s, "hgt", -1), shift(s, "hgt", 1)
    face = (HIGH, 4, HALO, LANES)
    edge, head, tail = call(
        edge_kernel, "edge", [(HIGH, WIDE, LANES), face, face], [from_right, from_left, s]
    )
    before = shift(tail, "wid", 1)
    after = shift(head, "wid", -1)
    rim = (HALF, RIM, LANES)
    low, top = call(rim_kernel, "rim", [rim, rim], [edge, before, after])
    over_rim, under_rim = shift(low, "hgt", -1), shift(top, "hgt", 1)
    state = pltpu.VMEM((2, TALL, COLS, 8, LANES), jnp.float32)
    depth = lax.axis_size("len")
    sides = lax.axis_size("wid") * lax.axis_size("hgt")
    split, traces = call(
        march_kernel,
        "march",
        [(HIGH, WIDE, LANES), (depth, STEPS, LANES)],
        [source_cells, source_signal, receiver_cells.T, s, edge, before, after]
        + [under, under_rim, over, over_rim],
        scratch=[
            state,
            state,
            state,
            pltpu.VMEM((4, BROAD, LANES), jnp.float32),
            pltpu.VMEM((LANES, STEPS, LANES), jnp.float32),
            pltpu.SMEM((8, LANES), jnp.int32),
        ],
        scalars=3,
        limit=LIMIT,
    )
    traces = lax.all_to_all(traces, "len", 0, 0, tiled=True)
    (traces,) = call(relay_kernel, "relay", [(sides, STEPS, LANES)], [traces])
    traces = lax.all_to_all(traces, ("wid", "hgt"), 0, 0, tiled=True)
    (now,) = call(order_kernel, "order", [(HIGH, WIDE, DEEP)], [split])
    return now, jnp.sum(traces, axis=0)


LIMIT = 32


def solution(mesh):
    block = P("hgt", "wid", "len")
    return jax.shard_map(
        per_device,
        mesh=mesh,
        in_specs=(block, block, block, P(), P(), P(), P()),
        out_specs=(block, P()),
        check_vma=False,
    )
```

```python
import functools

import jax
import jax.numpy as jnp
from jax import lax
from jax.experimental import pallas as pl
from jax.experimental.pallas import tpu as pltpu
from jax.sharding import PartitionSpec as P

STEPS = 16
HALO = 16
LANES = 128
HIGH, WIDE, DEEP = 16, 64, 128
HALF = HIGH // 2
TALL = HIGH + 2 * HALO
BROAD = WIDE + 2 * HALO
COLS = BROAD // 8
RIM = 3 * 2 * HALO + BROAD
VMEM = pl.BlockSpec(memory_space=pltpu.VMEM)
SMEM = pl.BlockSpec(memory_space=pltpu.SMEM)


def lane_ids():
    return lax.broadcasted_iota(jnp.int32, (8, LANES), 1)


def regroup(rows, order):
    return jnp.take_along_axis(rows, order, axis=1, mode="promise_in_bounds")


def even_odd():
    lane = lane_ids()
    return jnp.where(lane < 64, 2 * lane, 2 * lane - 127)


def in_order():
    lane = lane_ids()
    return (lane // 2) + 64 * (lane % 2)


def pack_kernel(
    adm_ref, now_ref, old_ref, cls_ref, s_ref, left_ref, right_ref, head_ref, tail_ref
):
    lane = lane_ids()
    order = even_odd()

    def layer(h, carry):
        rims = []
        for j in range(WIDE // 8):
            rows = pl.ds(8 * j, 8)
            kinds = cls_ref[h, rows, :]
            loss = jnp.zeros((8, LANES), jnp.float32)
            for index in range(adm_ref.shape[0]):
                loss = jnp.where(kinds == index + 1, adm_ref[index], loss)
            gain = jnp.float32(1.0 / 3.0) / (1.0 + loss)
            rim = None
            for a, field in enumerate((now_ref[h, rows, :], old_ref[h, rows, :], gain)):
                split = regroup(field, order)
                s_ref[h, a, rows, :] = split
                if j < HALO // 8:
                    head_ref[h, a, rows, :] = split
                if j >= (WIDE - HALO) // 8:
                    tail_ref[h, a, pl.ds(8 * j - WIDE + HALO, 8), :] = split
                moved = pltpu.roll(split, 72, 1)
                both = jnp.where((lane < 8) | ((lane >= 56) & (lane < 64)), split, moved)
                if a == 0:
                    rim = both
                else:
                    both = pltpu.roll(both, 16 * a, 1)
                    here = (lane >= 16 * a) & (lane < 16 * a + 16)
                    here = here | ((lane >= 56 + 16 * a) & (lane < 72 + 16 * a))
                    rim = jnp.where(here, both, rim)
            rims.append(rim)
        half = WIDE // 16
        for j in range(half):
            rows = pl.ds(8 * j, 8)
            other = pltpu.roll(rims[j + half], 64, 1)
            left_ref[h, rows, :] = jnp.where(lane < 56, rims[j], other)
            right_ref[h, rows, :] = jnp.where((lane >= 56) & (lane < 104), rims[j], other)
        return carry

    lax.fori_loop(0, HIGH, layer, 0)


def edge_kernel(from_right_ref, from_left_ref, e_ref, head_ref, tail_ref):
    lane = lane_ids()
    zero = jnp.float32(0.0)
    used = (lane < 48) | ((lane >= 56) & (lane < 104))

    def layer(h, carry):
        half = WIDE // 16
        for j in range(half):
            rows = pl.ds(8 * j, 8)
            a, b = from_right_ref[h, rows, :], from_left_ref[h, rows, :]
            first = jnp.where(lane < 48, a, b)
            second = pltpu.roll(jnp.where((lane >= 64) & (lane < 112), a, b), 64, 1)
            first = jnp.where(used, first, zero)
            second = jnp.where(used, second, zero)
            e_ref[h, rows, :] = first
            e_ref[h, pl.ds(8 * (j + half), 8), :] = second
            if j < HALO // 8:
                head_ref[h, rows, :] = first
            if j >= half - HALO // 8:
                tail_ref[h, pl.ds(8 * (j - half) + HALO, 8), :] = second
        return carry

    lax.fori_loop(0, HIGH, layer, 0)


def beside_lanes(i):
    lane = lane_ids()
    k = lane % 8
    n = (HALO - i) // 2
    right = lane < 48
    return right, n, (right & (k < n)) | (~right & (k >= 8 - n))


def rim_kernel(e_ref, before_ref, after_ref, before_e, after_e, low_ref, top_ref):
    row = lax.broadcasted_iota(jnp.int32, (HALO, LANES), 0)

    def pair(out_ref, i, near, far):
        for a in range(3):
            at = 2 * HALO * a
            kept = jnp.where(row > i, before_ref[near, a], pltpu.roll(before_ref[far, a], i, 0))
            out_ref[i, pl.ds(at, HALO), :] = kept
            moved = pltpu.roll(after_ref[far, a], (HALO - i) % HALO, 0)
            out_ref[i, pl.ds(at + HALO, HALO), :] = jnp.where(row < HALO - i - 1, after_ref[near, a], moved)
        right, n, mask = beside_lanes(i)
        for j in range(COLS):
            if j < HALO // 8:
                a, b = before_e[near, pl.ds(8 * j, 8), :], before_e[far, pl.ds(8 * j, 8), :]
            elif j < COLS - HALO // 8:
                at = 8 * j - HALO
                a, b = e_ref[near, pl.ds(at, 8), :], e_ref[far, pl.ds(at, 8), :]
            else:
                at = 8 * j - HALO - WIDE
                a, b = after_e[near, pl.ds(at, 8), :], after_e[far, pl.ds(at, 8), :]
            moved = jnp.where(right, pltpu.roll(b, n, 1), pltpu.roll(b, LANES - n, 1))
            out_ref[i, pl.ds(6 * HALO + 8 * j, 8), :] = jnp.where(mask, a, moved)

    def both(i, carry):
        pair(low_ref, i, i, HIGH - 1 - i)
        pair(top_ref, i, HIGH - 1 - i, i)
        return carry

    lax.fori_loop(0, HALF, both, 0)


def fill(refs, temp, at):
    lane = lane_ids()
    zero = jnp.float32(0.0)
    fringe = ((lane >= 64) & (lane < 72)) | (lane >= 120)
    for j in range(COLS):
        edge = temp[3, pl.ds(j, 8, stride=COLS), :]
        for a, ref in enumerate(refs):
            main = temp[a, pl.ds(j, 8, stride=COLS), :]
            for parity in range(2):
                near = pltpu.roll(edge, 64 - 8 * (2 * a + parity), 1)
                near = jnp.where(fringe, near, zero)
                mid = pltpu.roll(main, 64, 1) if parity else main
                ref[parity, at, j] = jnp.where(lane < 64, mid, near)


def fill_own(refs, temp, s_ref, e_ref, before_ref, after_ref, before_e, after_e):
    def layer(h, carry):
        for a in range(3):
            temp[a, pl.ds(HALO, WIDE), :] = s_ref[h, a]
            temp[a, pl.ds(0, HALO), :] = before_ref[h, a]
            temp[a, pl.ds(HALO + WIDE, HALO), :] = after_ref[h, a]
        temp[3, pl.ds(0, HALO), :] = before_e[h]
        temp[3, pl.ds(HALO, WIDE), :] = e_ref[h]
        temp[3, pl.ds(HALO + WIDE, HALO), :] = after_e[h]
        fill(refs, temp, h)
        return carry

    lax.fori_loop(0, HIGH, layer, 0)


def fill_beside(refs, temp, s_ref, rim_ref, layers):
    def pair(i, carry):
        near, far = layers(i)
        for a in range(3):
            temp[a, pl.ds(0, HALO), :] = rim_ref[i, pl.ds(2 * HALO * a, HALO), :]
            temp[a, pl.ds(HALO, WIDE), :] = s_ref[near % HIGH, a]
            temp[a, pl.ds(HALO + WIDE, HALO), :] = rim_ref[i, pl.ds(2 * HALO * a + HALO, HALO), :]
        temp[3] = rim_ref[i, pl.ds(6 * HALO, BROAD), :]
        fill(refs, temp, near)
        for a in range(3):
            before = rim_ref[i, pl.ds(2 * HALO * a, HALO), :]
            temp[a, pl.ds(0, HALO), :] = pltpu.roll(before, (HALO - i) % HALO, 0)
            temp[a, pl.ds(HALO, WIDE), :] = s_ref[far % HIGH, a]
            after = rim_ref[i, pl.ds(2 * HALO * a + HALO, HALO), :]
            temp[a, pl.ds(HALO + WIDE, HALO), :] = pltpu.roll(after, i, 0)
        right, n, _ = beside_lanes(i)
        k = lane_ids() % 8
        mask = (right & (k < 8 - n)) | (~right & (k >= n))
        for j in range(COLS):
            both = rim_ref[i, pl.ds(6 * HALO + 8 * j, 8), :]
            moved = jnp.where(right, pltpu.roll(both, LANES - n, 1), pltpu.roll(both, n, 1))
            temp[3, pl.ds(8 * j, 8), :] = jnp.where(mask, moved, jnp.float32(0.0))
        fill(refs, temp, far)
        return carry

    lax.fori_loop(0, HALF, pair, 0)


def corner():
    return (
        lax.axis_index("hgt") * HIGH - HALO,
        lax.axis_index("wid") * WIDE - HALO,
        lax.axis_index("len") * DEEP,
    )


def list_receivers(rec_ref, todo):
    start = corner()

    def note(r, count):
        h = rec_ref[0, r] - start[0]
        w = rec_ref[1, r] - start[1]
        d = rec_ref[2, r] - start[2]
        mine = (h >= HALO) & (h < HALO + HIGH) & (w >= HALO) & (w < HALO + WIDE)
        mine = mine & (d >= 0) & (d < DEEP)

        @pl.when(mine)
        def _():
            todo[0, count] = r
            todo[1, count] = h
            todo[2, count] = w % COLS
            todo[3, count] = w // COLS
            todo[4, count] = d % 2
            todo[5, count] = d // 2

        return count + mine.astype(jnp.int32)

    todo[6, 0] = lax.fori_loop(0, rec_ref.shape[1], note, jnp.int32(0))


def list_sources(src_ref):
    lane = lane_ids()
    row = lax.broadcasted_iota(jnp.int32, (8, LANES), 0)
    start = corner()
    points = []
    for s in range(src_ref.shape[0]):
        h = src_ref[s, 0] - start[0]
        w = src_ref[s, 1] - start[1]
        d = src_ref[s, 2] - start[2] + HALO
        near = (h >= 0) & (h < TALL) & (w >= 0) & (w < BROAD) & (d >= 0) & (d < DEEP + 2 * HALO)
        h = jnp.clip(h, 0, TALL - 1)
        w = jnp.clip(w, 0, BROAD - 1)
        d = jnp.clip(d, 0, DEEP + 2 * HALO - 1)
        place = (d // 2 + LANES - HALO // 2) % LANES
        points.append((near, d % 2, h, w % COLS, (row == w // COLS) & (lane == place)))
    return points


def sweep(now, old, p_ref, first, trips, layers):
    def chunk(i, carry):
        for u in range(layers):
            h = first(i) + u
            for parity in range(2):
                other = [now[1 - parity, h, j] for j in range(COLS)]
                mine = [now[parity, h, j] for j in range(COLS)]
                for j in range(COLS):
                    before = mine[j - 1] if j > 0 else pltpu.roll(mine[COLS - 1], 1, 0)
                    after = mine[j + 1] if j < COLS - 1 else pltpu.roll(mine[0], 7, 0)
                    beside = other[j] + pltpu.roll(other[j], 127 if parity else 1, 1)
                    total = (now[parity, h - 1, j] + now[parity, h + 1, j]) + (before + after)
                    total = total + beside
                    past = old[parity, h, j]
                    old[parity, h, j] = past + p_ref[parity, h, j] * (total - 6.0 * past)
        return carry

    lax.fori_loop(0, trips, chunk, 0)


def inject(field, points, sig_ref, t, base, inside):
    for s, (near, parity, h, j, spot) in enumerate(points):

        @pl.when(near & inside(h))
        def _():
            add = jnp.where(spot, sig_ref[s, t], jnp.float32(0.0))
            field[parity, h - base, j] = field[parity, h - base, j] + add


def keep(field, todo, hist, t, base):
    def one(i, carry):
        row = field[todo[4, i], todo[1, i] - base, todo[2, i], pl.ds(todo[3, i], 1), :]
        hist[i, pl.ds(t, 1), :] = row
        return carry

    lax.fori_loop(0, todo[6, 0], one, 0)


def gather(trace, todo, hist, early):
    lane = lax.broadcasted_iota(jnp.int32, (STEPS, LANES), 1)
    step = lax.broadcasted_iota(jnp.int32, (STEPS, LANES), 0)

    def one(i, carry):
        number, h = todo[0, i], todo[1, i]
        moved = pltpu.roll(hist[i], (number - todo[5, i] + LANES) % LANES, 1)
        done_early = (h > HALO + step) & (h < TALL - HALO - 1 - step)
        now = done_early if early else ~done_early
        trace[...] = jnp.where((lane == number) & now, moved, trace[...])
        return carry

    lax.fori_loop(0, todo[6, 0], one, 0)


def inner_kernel(src_ref, sig_ref, rec_ref, *refs):
    a_ref, b_ref, p_ref, trace_ref, todo, temp, hist = refs[6:]
    list_receivers(rec_ref, todo)
    fill_own((a_ref, b_ref, p_ref), temp, *refs[:6])
    points = list_sources(src_ref)

    def step(now, old, t):
        sweep(now, old, p_ref, lambda i: t + 1 + 2 * i, HALF - 1 - t, 2)
        inject(old, points, sig_ref, t, HALO, lambda h: (h > HALO + t) & (h < HALO + HIGH - 1 - t))
        keep(old, todo, hist, t, HALO)

    def pair(i, carry):
        step(a_ref, b_ref, 2 * i)
        step(b_ref, a_ref, 2 * i + 1)
        return carry

    lax.fori_loop(0, HALF // 2, pair, 0)
    trace_ref[...] = jnp.zeros((STEPS, LANES), jnp.float32)
    gather(trace_ref, todo, hist, True)


def march_kernel(src_ref, sig_ref, todo, *refs):
    own = refs[:3]
    early_ref, under, under_rim, over, over_rim = refs[3:8]
    out_ref, trace_ref = refs[8:10]
    a_ref, b_ref, p_ref, temp, hist = refs[10:]
    fields = (a_ref, b_ref, p_ref)

    def take(h, carry):
        for ref, got in zip(fields, own):
            for parity in range(2):
                ref[parity, HALO + h] = got[parity, h]
        return carry

    lax.fori_loop(0, HIGH, take, 0)
    fill_beside(fields, temp, under, under_rim, lambda i: (HALO - 1 - i, i))
    fill_beside(fields, temp, over, over_rim, lambda i: (HALO + HIGH + i, TALL - 1 - i))
    points = list_sources(src_ref)

    def step(now, old, t):
        early = t < HALF - 1
        full = TALL - 2 * (t + 1)
        fours = jnp.where(early, HIGH // 2, full // 4)
        gap = jnp.where(early, HIGH - 2 * (t + 1), 0)
        sweep(
            now,
            old,
            p_ref,
            lambda i: t + 1 + 4 * i + jnp.where(i >= HIGH // 4, gap, 0),
            fours,
            4,
        )
        sweep(now, old, p_ref, lambda i: t + 1 + 4 * fours, jnp.where(early, 0, (full % 4) // 2), 2)
        inject(old, points, sig_ref, t, 0, lambda h: (h <= HALO + t) | (h >= HALO + HIGH - 1 - t))
        keep(old, todo, hist, t, 0)

    def pair(i, carry):
        step(a_ref, b_ref, 2 * i)
        step(b_ref, a_ref, 2 * i + 1)
        return carry

    lax.fori_loop(0, STEPS // 2, pair, 0)

    trace_ref[0] = early_ref[...]
    gather(trace_ref.at[0], todo, hist, False)
    for i in range(1, trace_ref.shape[0]):
        trace_ref[i] = trace_ref[0]

    lane = lane_ids()
    plain = temp.at[0]

    def hand_on(h, carry):
        for j in range(COLS):
            even, odd = a_ref[0, HALO + h, j], a_ref[1, HALO + h, j]
            joined = jnp.where(lane < 64, even, pltpu.roll(odd, 64, 1))
            plain[pl.ds(j, 8, stride=COLS), :] = joined
        out_ref[h] = plain[pl.ds(HALO, WIDE), :]
        return carry

    lax.fori_loop(0, HIGH, hand_on, 0)


def order_kernel(split_ref, out_ref):
    order = in_order()

    def layer(h, carry):
        for j in range(WIDE // 8):
            rows = pl.ds(8 * j, 8)
            out_ref[h, rows, :] = regroup(split_ref[h, rows, :], order)
        return carry

    lax.fori_loop(0, split_ref.shape[0], layer, 0)


def relay_kernel(got_ref, out_ref):
    total = got_ref[0]
    for i in range(1, got_ref.shape[0]):
        total = total + got_ref[i]
    for i in range(out_ref.shape[0]):
        out_ref[i] = total


def field(*shape):
    return jax.ShapeDtypeStruct(shape, jnp.float32)


def call(kernel, name, outs, ins, scratch=(), scalars=0, limit=8, listed=False):
    out_shape = [field(*shape) for shape in outs]
    out_specs = [VMEM for _ in outs]
    if listed:
        out_shape.append(jax.ShapeDtypeStruct((8, LANES), jnp.int32))
        out_specs.append(SMEM)
    return pl.pallas_call(
        kernel,
        out_shape=tuple(out_shape),
        in_specs=[SMEM] * scalars + [VMEM] * (len(ins) - scalars),
        out_specs=tuple(out_specs),
        scratch_shapes=list(scratch),
        name=name,
        compiler_params=pltpu.CompilerParams(vmem_limit_bytes=limit << 20),
    )(*ins)


def shift(x, axis, move):
    size = lax.axis_size(axis)
    pairs = [(i, i + move) for i in range(size) if 0 <= i + move < size]
    return lax.ppermute(x, axis, pairs)


def per_device(
    pressure_now, pressure_old, classes, admittance, source_cells, source_signal, receiver_cells
):
    strip = (HIGH, WIDE // 2, LANES)
    face = (HIGH, 3, HALO, LANES)
    outs = [(HIGH, 3, WIDE, LANES), strip, strip, face, face]
    s, to_left, to_right, head, tail = call(
        pack_kernel, "pack", outs, [admittance, pressure_now, pressure_old, classes], scalars=1
    )
    from_right = shift(to_left, "len", -1)
    from_left = shift(to_right, "len", 1)
    before, after = shift(tail, "wid", 1), shift(head, "wid", -1)
    over, under = shift(s, "hgt", -1), shift(s, "hgt", 1)
    edge, head, tail = call(
        edge_kernel,
        "edge",
        [(HIGH, WIDE, LANES), (HIGH, HALO, LANES), (HIGH, HALO, LANES)],
        [from_right, from_left],
    )
    head, tail, before, after = lax.optimization_barrier((head, tail, before, after))
    before_e, after_e = shift(tail, "wid", 1), shift(head, "wid", -1)
    rim = (HALF, RIM, LANES)
    low, top = call(rim_kernel, "rim", [rim, rim], [edge, before, after, before_e, after_e])
    over_rim, under_rim = shift(low, "hgt", -1), shift(top, "hgt", 1)
    own = (2, HIGH, COLS, 8, LANES)
    temp = pltpu.VMEM((4, BROAD, LANES), jnp.float32)
    hist = pltpu.VMEM((LANES, STEPS, LANES), jnp.float32)
    now, old, gain, early, todo = call(
        inner_kernel,
        "inner",
        [own, own, own, (STEPS, LANES)],
        [source_cells, source_signal.T, receiver_cells.T]
        + [s, edge, before, after, before_e, after_e],
        scratch=[temp, hist],
        scalars=3,
        limit=8,
        listed=True,
    )
    state = pltpu.VMEM((2, TALL, COLS, 8, LANES), jnp.float32)
    depth = lax.axis_size("len")
    sides = lax.axis_size("wid") * lax.axis_size("hgt")
    split, traces = call(
        march_kernel,
        "march",
        [(HIGH, WIDE, LANES), (depth, STEPS, LANES)],
        [source_cells, source_signal.T, todo, now, old, gain, early]
        + [under, under_rim, over, over_rim],
        scratch=[state, state, state, temp, hist],
        scalars=3,
        limit=20,
    )
    traces = lax.all_to_all(traces, "len", 0, 0, tiled=True)
    (traces,) = call(relay_kernel, "relay", [(sides, STEPS, LANES)], [traces])
    traces = lax.all_to_all(traces, ("wid", "hgt"), 0, 0, tiled=True)
    (now,) = call(order_kernel, "order", [(HIGH, WIDE, DEEP)], [split])
    return now, jnp.sum(traces, axis=0)


def solution(mesh):
    block = P("hgt", "wid", "len")
    return jax.shard_map(
        per_device,
        mesh=mesh,
        in_specs=(block, block, block, P(), P(), P(), P()),
        out_specs=(block, P()),
        check_vma=False,
    )
```

```python
import functools

import jax
import jax.numpy as jnp
from jax import lax
from jax.experimental import pallas as pl
from jax.experimental.pallas import tpu as pltpu
from jax.sharding import PartitionSpec as P

STEPS = 16
HALO = 16
LANES = 128
HIGH, WIDE, DEEP = 16, 64, 128
HALF = HIGH // 2
TALL = HIGH + 2 * HALO
BROAD = WIDE + 2 * HALO
COLS = BROAD // 8
VMEM = pl.BlockSpec(memory_space=pltpu.VMEM)
SMEM = pl.BlockSpec(memory_space=pltpu.SMEM)


def lane_ids():
    return lax.broadcasted_iota(jnp.int32, (8, LANES), 1)


def regroup(rows, order):
    return jnp.take_along_axis(rows, order, axis=1, mode="promise_in_bounds")


def even_odd():
    lane = lane_ids()
    return jnp.where(lane < 64, 2 * lane, 2 * lane - 127)


def in_order():
    lane = lane_ids()
    return (lane // 2) + 64 * (lane % 2)


def pack_kernel(adm_ref, now_ref, old_ref, cls_ref, s_ref, head_ref, tail_ref):
    order = even_odd()

    def layer(h, carry):
        for j in range(WIDE // 8):
            rows = pl.ds(8 * j, 8)
            kinds = cls_ref[h, rows, :]
            loss = jnp.zeros((8, LANES), jnp.float32)
            for index in range(adm_ref.shape[0]):
                loss = jnp.where(kinds == index + 1, adm_ref[index], loss)
            gain = jnp.float32(1.0 / 3.0) / (1.0 + loss)
            for a, field in enumerate((now_ref[h, rows, :], old_ref[h, rows, :], gain)):
                split = regroup(field, order)
                s_ref[h, a, rows, :] = split
                if j < HALO // 8:
                    head_ref[h, a, rows, :] = split
                if j >= (WIDE - HALO) // 8:
                    tail_ref[h, a, pl.ds(8 * j - WIDE + HALO, 8), :] = split
        return carry

    lax.fori_loop(0, HIGH, layer, 0)


def face_lanes(fields):
    lane = lane_ids()
    out = None
    for a, split in enumerate(fields):
        moved = pltpu.roll(split, 72, 1)
        both = jnp.where((lane < 8) | ((lane >= 56) & (lane < 64)), split, moved)
        if a == 0:
            out = both
        else:
            both = pltpu.roll(both, 16 * a, 1)
            here = (lane >= 16 * a) & (lane < 16 * a + 16)
            here = here | ((lane >= 56 + 16 * a) & (lane < 72 + 16 * a))
            out = jnp.where(here, both, out)
    return out


def own_strip_kernel(rec_ref, s_ref, strip_ref, todo):
    list_receivers(rec_ref, todo)

    def layer(h, carry):
        for j in range(WIDE // 8):
            rows = pl.ds(8 * j, 8)
            strip_ref[h, rows, :] = face_lanes([s_ref[h, a, rows, :] for a in range(3)])
        return carry

    lax.fori_loop(0, HIGH, layer, 0, unroll=4)


def strip_kernel(strip_ref, before_ref, after_ref, left_ref, right_ref):
    lane = lane_ids()
    k = lane % 8
    inner = HALO // 2
    rim = face_lanes

    def layer(h, carry):
        low, high = pl.ds(0, inner), pl.ds(inner, inner)
        rims = [rim([before_ref[h, a, high, :] for a in range(3)])]
        for j in range(WIDE // 8):
            rims.append(strip_ref[h, pl.ds(8 * j, 8), :])
        rims.append(rim([after_ref[h, a, low, :] for a in range(3)]))
        one = rim([before_ref[h, a, low, :] for a in range(3)])
        two = rim([after_ref[h, a, high, :] for a in range(3)])
        heads = jnp.where(k < 4, one, pltpu.roll(two, 4, 1))
        tails = jnp.where(k >= 4, one, pltpu.roll(two, LANES - 4, 1))
        outer = jnp.where(lane < 48, heads, tails)
        half = len(rims) // 2
        for j in range(half):
            rows = pl.ds(8 * j, 8)
            other = pltpu.roll(rims[j + half], 64, 1)
            left = jnp.where(lane < 56, rims[j], other)
            right = jnp.where((lane >= 56) & (lane < 104), rims[j], other)
            if j < 3:
                spare = pltpu.roll(outer, 48 - 16 * j, 1)
                left = jnp.where((lane >= 48) & (lane < 64), spare, left)
                right = jnp.where((lane >= 104) & (lane < 120), spare, right)
            left_ref[h, rows, :] = left
            right_ref[h, rows, :] = right
        return carry

    lax.fori_loop(0, HIGH, layer, 0, unroll=4)


def beside_lanes(i):
    lane = lane_ids()
    k = lane % 8
    n = (HALO - i) // 2
    right = (lane >= 64) & (lane < 112)
    return right, n, (right & (k < n)) | (~right & (k >= 8 - n))


def wide_rim_kernel(before_ref, after_ref, low_ref, top_ref):
    row = lax.broadcasted_iota(jnp.int32, (HALO, LANES), 0)

    def pair(out_ref, i, near, far):
        for a in range(3):
            at = 2 * HALO * a
            kept = jnp.where(row > i, before_ref[near, a], pltpu.roll(before_ref[far, a], i, 0))
            out_ref[i, pl.ds(at, HALO), :] = kept
            moved = pltpu.roll(after_ref[far, a], (HALO - i) % HALO, 0)
            kept = jnp.where(row < HALO - i - 1, after_ref[near, a], moved)
            out_ref[i, pl.ds(at + HALO, HALO), :] = kept

    def both(i, carry):
        pair(low_ref, i, i, HIGH - 1 - i)
        pair(top_ref, i, HIGH - 1 - i, i)
        return carry

    lax.fori_loop(0, HALF, both, 0)


def long_rim_kernel(from_right_ref, from_left_ref, e_ref, low_ref, top_ref):
    lane = lane_ids()
    zero = jnp.float32(0.0)
    unused = ((lane >= 40) & (lane < 64)) | ((lane >= 112) & (lane < 120))

    rights = (lane >= 64) & (lane < 112)
    k = lane % 8
    nearest = (rights & (k < 4)) | (~rights & (k >= 4))

    def unfold(h, carry):
        half = (BROAD - HALO) // 16
        outer = zero
        for j in range(half):
            a, b = from_right_ref[h, pl.ds(8 * j, 8), :], from_left_ref[h, pl.ds(8 * j, 8), :]
            first = pltpu.roll(jnp.where(lane < 48, a, b), 64, 1)
            second = jnp.where(rights, a, b)
            at = HALO // 2 + 8 * j
            e_ref[h, pl.ds(at, 8), :] = jnp.where(unused, zero, first)
            e_ref[h, pl.ds(at + 8 * half, 8), :] = jnp.where(unused, zero, second)
            if j < 3:
                spare = pltpu.roll(jnp.where((lane >= 48) & (lane < 64), a, b), 16 + 16 * j, 1)
                here = (lane >= 64 + 16 * j) & (lane < 80 + 16 * j)
                start = (120 + 16 * j) % LANES
                if j == 0:
                    here = here | (lane >= start) | (lane < 8)
                else:
                    here = here | ((lane >= start) & (lane < start + 16))
                outer = jnp.where(here, spare, outer)
        one = jnp.where(nearest, outer, zero)
        two = jnp.where(rights, pltpu.roll(outer, LANES - 4, 1), pltpu.roll(outer, 4, 1))
        e_ref[h, pl.ds(0, 8), :] = jnp.where(unused, zero, one)
        e_ref[h, pl.ds(BROAD - 8, 8), :] = jnp.where(unused | ~nearest, zero, two)
        return carry

    lax.fori_loop(0, HIGH, unfold, 0, unroll=4)

    def pair(out_ref, i, near, far):
        right, n, mask = beside_lanes(i)
        for j in range(COLS):
            a, b = e_ref[near, pl.ds(8 * j, 8), :], e_ref[far, pl.ds(8 * j, 8), :]
            moved = jnp.where(right, pltpu.roll(b, n, 1), pltpu.roll(b, LANES - n, 1))
            out_ref[i, pl.ds(8 * j, 8), :] = jnp.where(mask, a, moved)

    def both(i, carry):
        pair(low_ref, i, i, HIGH - 1 - i)
        pair(top_ref, i, HIGH - 1 - i, i)
        return carry

    lax.fori_loop(0, HALF, both, 0, unroll=2)


def fill(refs, temp, at):
    lane = lane_ids()
    zero = jnp.float32(0.0)
    fringe = ((lane >= 64) & (lane < 72)) | (lane >= 120)
    for j in range(COLS):
        edge = temp[3, pl.ds(j, 8, stride=COLS), :]
        for a, ref in enumerate(refs):
            main = temp[a, pl.ds(j, 8, stride=COLS), :]
            for parity in range(2):
                turn = 8 * (2 * a + parity)
                near = pltpu.roll(edge, LANES - turn, 1) if turn else edge
                near = jnp.where(fringe, near, zero)
                mid = pltpu.roll(main, 64, 1) if parity else main
                ref[parity, at, j] = jnp.where(lane < 64, mid, near)


def fill_own(refs, temp, s_ref, e_ref, before_ref, after_ref):
    def layer(h, carry):
        for a in range(3):
            temp[a, pl.ds(HALO, WIDE), :] = s_ref[h, a]
            temp[a, pl.ds(0, HALO), :] = before_ref[h, a]
            temp[a, pl.ds(HALO + WIDE, HALO), :] = after_ref[h, a]
        temp[3] = e_ref[h]
        fill(refs, temp, h)
        return carry

    lax.fori_loop(0, HIGH, layer, 0)


def fill_beside(refs, temp, s_ref, rim_ref, edge_ref, layers):
    def pair(i, carry):
        near, far = layers(i)
        for a in range(3):
            temp[a, pl.ds(0, HALO), :] = rim_ref[i, pl.ds(2 * HALO * a, HALO), :]
            temp[a, pl.ds(HALO, WIDE), :] = s_ref[near % HIGH, a]
            temp[a, pl.ds(HALO + WIDE, HALO), :] = rim_ref[i, pl.ds(2 * HALO * a + HALO, HALO), :]
        temp[3] = edge_ref[i]
        fill(refs, temp, near)
        for a in range(3):
            before = rim_ref[i, pl.ds(2 * HALO * a, HALO), :]
            temp[a, pl.ds(0, HALO), :] = pltpu.roll(before, (HALO - i) % HALO, 0)
            temp[a, pl.ds(HALO, WIDE), :] = s_ref[far % HIGH, a]
            after = rim_ref[i, pl.ds(2 * HALO * a + HALO, HALO), :]
            temp[a, pl.ds(HALO + WIDE, HALO), :] = pltpu.roll(after, i, 0)
        right, n, _ = beside_lanes(i)
        k = lane_ids() % 8
        mask = (right & (k < 8 - n)) | (~right & (k >= n))
        for j in range(COLS):
            both = edge_ref[i, pl.ds(8 * j, 8), :]
            moved = jnp.where(right, pltpu.roll(both, LANES - n, 1), pltpu.roll(both, n, 1))
            temp[3, pl.ds(8 * j, 8), :] = jnp.where(mask, moved, jnp.float32(0.0))
        fill(refs, temp, far)
        return carry

    lax.fori_loop(0, HALF, pair, 0)


def corner():
    return (
        lax.axis_index("hgt") * HIGH - HALO,
        lax.axis_index("wid") * WIDE - HALO,
        lax.axis_index("len") * DEEP,
    )


def list_receivers(rec_ref, todo):
    start = corner()

    def note(r, count):
        h = rec_ref[0, r] - start[0]
        w = rec_ref[1, r] - start[1]
        d = rec_ref[2, r] - start[2]
        mine = (h >= HALO) & (h < HALO + HIGH) & (w >= HALO) & (w < HALO + WIDE)
        mine = mine & (d >= 0) & (d < DEEP)

        @pl.when(mine)
        def _():
            todo[0, count] = r
            todo[1, count] = h
            todo[2, count] = w % COLS
            todo[3, count] = w // COLS
            todo[4, count] = d % 2
            todo[5, count] = d // 2

        return count + mine.astype(jnp.int32)

    todo[6, 0] = lax.fori_loop(0, rec_ref.shape[1], note, jnp.int32(0), unroll=8)


def list_sources(src_ref):
    lane = lane_ids()
    row = lax.broadcasted_iota(jnp.int32, (8, LANES), 0)
    start = corner()
    points = []
    for s in range(src_ref.shape[0]):
        h = src_ref[s, 0] - start[0]
        w = src_ref[s, 1] - start[1]
        d = src_ref[s, 2] - start[2] + HALO
        near = (h >= 0) & (h < TALL) & (w >= 0) & (w < BROAD) & (d >= 0) & (d < DEEP + 2 * HALO)
        h = jnp.clip(h, 0, TALL - 1)
        w = jnp.clip(w, 0, BROAD - 1)
        d = jnp.clip(d, 0, DEEP + 2 * HALO - 1)
        place = (d // 2 + LANES - HALO // 2) % LANES
        points.append((near, d % 2, h, w % COLS, (row == w // COLS) & (lane == place)))
    return points


def sweep(now, old, p_ref, first, trips, layers):
    def chunk(i, carry):
        for u in range(layers):
            h = first(i) + u
            for part in range(2):
                js = range(part * COLS // 2, (part + 1) * COLS // 2)
                for parity in range(2):
                    side = {j: now[1 - parity, h, j] for j in js}
                    rolled = {j: pltpu.roll(side[j], 127 if parity else 1, 1) for j in js}
                    near = range(max(js[0] - 1, 0), min(js[-1] + 2, COLS))
                    mine = {j: now[parity, h, j] for j in near}
                    if part == 0:
                        mine[-1] = pltpu.roll(now[parity, h, COLS - 1], 1, 0)
                    else:
                        mine[COLS] = pltpu.roll(now[parity, h, 0], 7, 0)
                    known = {}
                    for j in js:
                        past = old[parity, h, j]
                        total = now[parity, h - 1, j] + now[parity, h + 1, j]
                        total = total + (mine[j - 1] + mine[j + 1]) + side[j]
                        known[j] = (past, total - 6.0 * past)
                    for j in js:
                        past, total = known[j]
                        old[parity, h, j] = past + p_ref[parity, h, j] * (total + rolled[j])
        return carry

    lax.fori_loop(0, trips, chunk, 0)


def inject(field, points, sig_ref, t, base, inside):
    for s, (near, parity, h, j, spot) in enumerate(points):

        @pl.when(near & inside(h))
        def _():
            add = jnp.where(spot, sig_ref[s, t], jnp.float32(0.0))
            field[parity, h - base, j] = field[parity, h - base, j] + add


def keep(field, todo, hist, t, base):
    def one(i, carry):
        row = field[todo[4, i], todo[1, i] - base, todo[2, i], pl.ds(todo[3, i], 1), :]
        hist[i, pl.ds(t, 1), :] = row
        return carry

    lax.fori_loop(0, todo[6, 0], one, 0)


def gather(trace, todo, hist, early):
    lane = lax.broadcasted_iota(jnp.int32, (STEPS, LANES), 1)
    step = lax.broadcasted_iota(jnp.int32, (STEPS, LANES), 0)

    def one(i, carry):
        number, h = todo[0, i], todo[1, i]
        moved = pltpu.roll(hist[i], (number - todo[5, i] + LANES) % LANES, 1)
        done_early = (h > HALO + step) & (h < TALL - HALO - 1 - step)
        now = done_early if early else ~done_early
        trace[...] = jnp.where((lane == number) & now, moved, trace[...])
        return carry

    lax.fori_loop(0, todo[6, 0], one, 0)


def inner_kernel(src_ref, sig_ref, todo, *refs):
    a_ref, b_ref, p_ref, trace_ref, temp, hist = refs[4:]
    fill_own((a_ref, b_ref, p_ref), temp, *refs[:4])
    points = list_sources(src_ref)

    def step(now, old, t):
        sweep(now, old, p_ref, lambda i: t + 1 + 2 * i, HALF - 1 - t, 2)
        inject(old, points, sig_ref, t, HALO, lambda h: (h > HALO + t) & (h < HALO + HIGH - 1 - t))
        keep(old, todo, hist, t, HALO)

    def pair(i, carry):
        step(a_ref, b_ref, 2 * i)
        step(b_ref, a_ref, 2 * i + 1)
        return carry

    lax.fori_loop(0, HALF // 2, pair, 0)
    trace_ref[...] = jnp.zeros((STEPS, LANES), jnp.float32)
    gather(trace_ref, todo, hist, True)


def march_kernel(src_ref, sig_ref, todo, *refs):
    own = refs[:3]
    early_ref, under, over = refs[3], refs[4:7], refs[7:10]
    out_ref, trace_ref = refs[10:12]
    a_ref, b_ref, p_ref, temp, hist = refs[12:]
    fields = (a_ref, b_ref, p_ref)

    def take(h, carry):
        for ref, got in zip(fields, own):
            for parity in range(2):
                ref[parity, HALO + h] = got[parity, h]
        return carry

    lax.fori_loop(0, HIGH, take, 0)
    fill_beside(fields, temp, *under, lambda i: (HALO - 1 - i, i))
    fill_beside(fields, temp, *over, lambda i: (HALO + HIGH + i, TALL - 1 - i))
    points = list_sources(src_ref)

    def step(now, old, t):
        early = t < HALF - 1
        full = TALL - 2 * (t + 1)
        fours = jnp.where(early, HIGH // 2, full // 4)
        gap = jnp.where(early, HIGH - 2 * (t + 1), 0)
        sweep(
            now,
            old,
            p_ref,
            lambda i: t + 1 + 4 * i + jnp.where(i >= HIGH // 4, gap, 0),
            fours,
            4,
        )
        sweep(now, old, p_ref, lambda i: t + 1 + 4 * fours, jnp.where(early, 0, (full % 4) // 2), 2)
        inject(old, points, sig_ref, t, 0, lambda h: (h <= HALO + t) | (h >= HALO + HIGH - 1 - t))
        keep(old, todo, hist, t, 0)

    def pair(i, carry):
        step(a_ref, b_ref, 2 * i)
        step(b_ref, a_ref, 2 * i + 1)
        return carry

    lax.fori_loop(0, STEPS // 2, pair, 0)

    trace_ref[0] = early_ref[...]
    gather(trace_ref.at[0], todo, hist, False)
    for i in range(1, trace_ref.shape[0]):
        trace_ref[i] = trace_ref[0]

    lane = lane_ids()
    plain = temp.at[0]

    def hand_on(h, carry):
        for j in range(COLS):
            even, odd = a_ref[0, HALO + h, j], a_ref[1, HALO + h, j]
            joined = jnp.where(lane < 64, even, pltpu.roll(odd, 64, 1))
            plain[pl.ds(j, 8, stride=COLS), :] = joined
        out_ref[h] = plain[pl.ds(HALO, WIDE), :]
        return carry

    lax.fori_loop(0, HIGH, hand_on, 0, unroll=4)


def order_kernel(split_ref, out_ref):
    order = in_order()

    def layer(h, carry):
        for j in range(WIDE // 8):
            rows = pl.ds(8 * j, 8)
            out_ref[h, rows, :] = regroup(split_ref[h, rows, :], order)
        return carry

    lax.fori_loop(0, split_ref.shape[0], layer, 0)


def relay_kernel(got_ref, out_ref):
    total = got_ref[0]
    for i in range(1, got_ref.shape[0]):
        total = total + got_ref[i]
    for i in range(out_ref.shape[0]):
        out_ref[i] = total


def field(*shape):
    return jax.ShapeDtypeStruct(shape, jnp.float32)


def call(kernel, name, outs, ins, scratch=(), scalars=0, limit=8, listed=False):
    out_shape = [field(*shape) for shape in outs]
    out_specs = [VMEM for _ in outs]
    if listed:
        out_shape.append(jax.ShapeDtypeStruct((8, LANES), jnp.int32))
        out_specs.append(SMEM)
    return pl.pallas_call(
        kernel,
        out_shape=tuple(out_shape),
        in_specs=[SMEM] * scalars + [VMEM] * (len(ins) - scalars),
        out_specs=tuple(out_specs),
        scratch_shapes=list(scratch),
        name=name,
        compiler_params=pltpu.CompilerParams(vmem_limit_bytes=limit << 20),
    )(*ins)


def shift(x, axis, move):
    size = lax.axis_size(axis)
    pairs = [(i, i + move) for i in range(size) if 0 <= i + move < size]
    return lax.ppermute(x, axis, pairs)


def per_device(
    pressure_now, pressure_old, classes, admittance, source_cells, source_signal, receiver_cells
):
    face = (HIGH, 3, HALO, LANES)
    s, head, tail = call(
        pack_kernel,
        "pack",
        [(HIGH, 3, WIDE, LANES), face, face],
        [admittance, pressure_now, pressure_old, classes],
        scalars=1,
    )
    over, under = shift(s, "hgt", -1), shift(s, "hgt", 1)
    before, after = shift(tail, "wid", 1), shift(head, "wid", -1)
    strip = (HIGH, (BROAD - HALO) // 2, LANES)
    mine, todo = call(
        own_strip_kernel,
        "own_strip",
        [(HIGH, WIDE, LANES)],
        [receiver_cells.T, s],
        scalars=1,
        listed=True,
    )
    before, after, mine = lax.optimization_barrier((before, after, mine))
    to_left, to_right = call(strip_kernel, "strip", [strip, strip], [mine, before, after])
    from_right = shift(to_left, "len", -1)
    from_left = shift(to_right, "len", 1)
    wide_rim, long_rim = (HALF, 3 * 2 * HALO, LANES), (HALF, BROAD, LANES)
    low, top = call(wide_rim_kernel, "wide_rim", [wide_rim, wide_rim], [before, after])
    over_rim, under_rim = shift(low, "hgt", -1), shift(top, "hgt", 1)
    edge, low, top = call(
        long_rim_kernel,
        "long_rim",
        [(HIGH, BROAD, LANES), long_rim, long_rim],
        [from_right, from_left],
    )
    over_edge, under_edge = shift(low, "hgt", -1), shift(top, "hgt", 1)
    own = (2, HIGH, COLS, 8, LANES)
    temp = pltpu.VMEM((4, BROAD, LANES), jnp.float32)
    hist = pltpu.VMEM((LANES, STEPS, LANES), jnp.float32)
    now, old, gain, early = call(
        inner_kernel,
        "inner",
        [own, own, own, (STEPS, LANES)],
        [source_cells, source_signal.T, todo]
        + [s, edge, before, after],
        scratch=[temp, hist],
        scalars=3,
        limit=8,
    )
    state = pltpu.VMEM((2, TALL, COLS, 8, LANES), jnp.float32)
    depth = lax.axis_size("len")
    sides = lax.axis_size("wid") * lax.axis_size("hgt")
    split, traces = call(
        march_kernel,
        "march",
        [(HIGH, WIDE, LANES), (depth, STEPS, LANES)],
        [source_cells, source_signal.T, todo, now, old, gain, early]
        + [under, under_rim, under_edge, over, over_rim, over_edge],
        scratch=[state, state, state, temp, hist],
        scalars=3,
        limit=20,
    )
    traces = lax.all_to_all(traces, "len", 0, 0, tiled=True)
    (traces,) = call(relay_kernel, "relay", [(sides, STEPS, LANES)], [traces])
    traces = lax.all_to_all(traces, ("wid", "hgt"), 0, 0, tiled=True)
    (now,) = call(order_kernel, "order", [(HIGH, WIDE, DEEP)], [split])
    return now, jnp.sum(traces, axis=0)


def solution(mesh):
    block = P("hgt", "wid", "len")
    return jax.shard_map(
        per_device,
        mesh=mesh,
        in_specs=(block, block, block, P(), P(), P(), P()),
        out_specs=(block, P()),
        check_vma=False,
    )
```

```python
import functools

import jax
import jax.numpy as jnp
from jax import lax
from jax.experimental import pallas as pl
from jax.experimental.pallas import tpu as pltpu
from jax.sharding import PartitionSpec as P

STEPS = 16
HALO = 16
LANES = 128
HIGH, WIDE, DEEP = 16, 64, 128
HALF = HIGH // 2
TALL = HIGH + 2 * HALO
BROAD = WIDE + 2 * HALO
COLS = BROAD // 8
VMEM = pl.BlockSpec(memory_space=pltpu.VMEM)
SMEM = pl.BlockSpec(memory_space=pltpu.SMEM)
HBM = pl.BlockSpec(memory_space=pltpu.HBM)
PARTS = 4
PACK_LIMIT = 60 << 20


def lane_ids():
    return lax.broadcasted_iota(jnp.int32, (8, LANES), 1)


def regroup(rows, order):
    return jnp.take_along_axis(rows, order, axis=1, mode="promise_in_bounds")


def even_odd():
    lane = lane_ids()
    return jnp.where(lane < 64, 2 * lane, 2 * lane - 127)


def in_order():
    lane = lane_ids()
    return (lane // 2) + 64 * (lane % 2)


def pack_kernel(
    adm_hbm, now_hbm, old_hbm, cls_hbm, s_hbm, head_hbm, tail_hbm,
    adm_ref, now_ref, old_ref, cls_ref, s_ref, head_ref, tail_ref, sems, out_sems, one_sem
):
    order = even_odd()

    def layer(h, carry):
        for j in range(WIDE // 8):
            rows = pl.ds(8 * j, 8)
            kinds = cls_ref[h, rows, :]
            loss = jnp.zeros((8, LANES), jnp.float32)
            for index in range(adm_ref.shape[0]):
                loss = jnp.where(kinds == index + 1, adm_ref[index], loss)
            gain = jnp.float32(1.0 / 3.0) / (1.0 + loss)
            for a, field in enumerate((now_ref[h, rows, :], old_ref[h, rows, :], gain)):
                split = regroup(field, order)
                s_ref[h, a, rows, :] = split
                if j < HALO // 8:
                    head_ref[h, a, rows, :] = split
                if j >= (WIDE - HALO) // 8:
                    tail_ref[h, a, pl.ds(8 * j - WIDE + HALO, 8), :] = split
        return carry

    layers = HIGH // PARTS
    fields = ((cls_hbm, cls_ref), (now_hbm, now_ref), (old_hbm, old_ref))
    single = pltpu.make_async_copy(adm_hbm, adm_ref, one_sem)
    single.start()
    copies = []
    for part in range(PARTS):
        at = pl.ds(part * layers, layers)
        for n, (src, dst) in enumerate(fields):
            copy = pltpu.make_async_copy(src.at[at], dst.at[at], sems.at[part, n])
            copy.start()
            copies.append(copy)
    results = ((s_ref, s_hbm), (head_ref, head_hbm), (tail_ref, tail_hbm))
    last = []
    single.wait()
    for part in range(PARTS):
        for copy in copies[3 * part : 3 * part + 3]:
            copy.wait()
        lax.fori_loop(part * layers, (part + 1) * layers, layer, 0)
        at = pl.ds(part * layers, layers)
        for n, (src, dst) in enumerate(results):
            copy = pltpu.make_async_copy(src.at[at], dst.at[at], out_sems.at[part, n])
            copy.start()
            last.append(copy)
    for copy in last:
        copy.wait()


def face_lanes(fields):
    lane = lane_ids()
    out = None
    for a, split in enumerate(fields):
        moved = pltpu.roll(split, 72, 1)
        both = jnp.where((lane < 8) | ((lane >= 56) & (lane < 64)), split, moved)
        if a == 0:
            out = both
        else:
            both = pltpu.roll(both, 16 * a, 1)
            here = (lane >= 16 * a) & (lane < 16 * a + 16)
            here = here | ((lane >= 56 + 16 * a) & (lane < 72 + 16 * a))
            out = jnp.where(here, both, out)
    return out


def own_strip_kernel(rec_ref, s_ref, strip_ref, todo):
    list_receivers(rec_ref, todo)

    def layer(h, carry):
        for j in range(WIDE // 8):
            rows = pl.ds(8 * j, 8)
            strip_ref[h, rows, :] = face_lanes([s_ref[h, a, rows, :] for a in range(3)])
        return carry

    lax.fori_loop(0, HIGH, layer, 0, unroll=4)


def strip_kernel(strip_ref, before_ref, after_ref, left_ref, right_ref):
    lane = lane_ids()
    k = lane % 8
    inner = HALO // 2
    rim = face_lanes

    def layer(h, carry):
        low, high = pl.ds(0, inner), pl.ds(inner, inner)
        rims = [rim([before_ref[h, a, high, :] for a in range(3)])]
        for j in range(WIDE // 8):
            rims.append(strip_ref[h, pl.ds(8 * j, 8), :])
        rims.append(rim([after_ref[h, a, low, :] for a in range(3)]))
        one = rim([before_ref[h, a, low, :] for a in range(3)])
        two = rim([after_ref[h, a, high, :] for a in range(3)])
        heads = jnp.where(k < 4, one, pltpu.roll(two, 4, 1))
        tails = jnp.where(k >= 4, one, pltpu.roll(two, LANES - 4, 1))
        outer = jnp.where(lane < 48, heads, tails)
        half = len(rims) // 2
        for j in range(half):
            rows = pl.ds(8 * j, 8)
            other = pltpu.roll(rims[j + half], 64, 1)
            left = jnp.where(lane < 56, rims[j], other)
            right = jnp.where((lane >= 56) & (lane < 104), rims[j], other)
            if j < 3:
                spare = pltpu.roll(outer, 48 - 16 * j, 1)
                left = jnp.where((lane >= 48) & (lane < 64), spare, left)
                right = jnp.where((lane >= 104) & (lane < 120), spare, right)
            left_ref[h, rows, :] = left
            right_ref[h, rows, :] = right
        return carry

    lax.fori_loop(0, HIGH, layer, 0, unroll=4)


def beside_lanes(i):
    lane = lane_ids()
    k = lane % 8
    n = (HALO - i) // 2
    right = (lane >= 64) & (lane < 112)
    return right, n, (right & (k < n)) | (~right & (k >= 8 - n))


def wide_rim_kernel(before_ref, after_ref, low_ref, top_ref):
    row = lax.broadcasted_iota(jnp.int32, (HALO, LANES), 0)

    def pair(out_ref, i, near, far):
        for a in range(3):
            at = 2 * HALO * a
            kept = jnp.where(row > i, before_ref[near, a], pltpu.roll(before_ref[far, a], i, 0))
            out_ref[i, pl.ds(at, HALO), :] = kept
            moved = pltpu.roll(after_ref[far, a], (HALO - i) % HALO, 0)
            kept = jnp.where(row < HALO - i - 1, after_ref[near, a], moved)
            out_ref[i, pl.ds(at + HALO, HALO), :] = kept

    def both(i, carry):
        pair(low_ref, i, i, HIGH - 1 - i)
        pair(top_ref, i, HIGH - 1 - i, i)
        return carry

    lax.fori_loop(0, HALF, both, 0)


def long_rim_kernel(from_right_ref, from_left_ref, e_ref, low_ref, top_ref):
    lane = lane_ids()
    zero = jnp.float32(0.0)
    unused = ((lane >= 40) & (lane < 64)) | ((lane >= 112) & (lane < 120))

    rights = (lane >= 64) & (lane < 112)
    k = lane % 8
    nearest = (rights & (k < 4)) | (~rights & (k >= 4))

    def unfold(h, carry):
        half = (BROAD - HALO) // 16
        outer = zero
        for j in range(half):
            a, b = from_right_ref[h, pl.ds(8 * j, 8), :], from_left_ref[h, pl.ds(8 * j, 8), :]
            first = pltpu.roll(jnp.where(lane < 48, a, b), 64, 1)
            second = jnp.where(rights, a, b)
            at = HALO // 2 + 8 * j
            e_ref[h, pl.ds(at, 8), :] = jnp.where(unused, zero, first)
            e_ref[h, pl.ds(at + 8 * half, 8), :] = jnp.where(unused, zero, second)
            if j < 3:
                spare = pltpu.roll(jnp.where((lane >= 48) & (lane < 64), a, b), 16 + 16 * j, 1)
                here = (lane >= 64 + 16 * j) & (lane < 80 + 16 * j)
                start = (120 + 16 * j) % LANES
                if j == 0:
                    here = here | (lane >= start) | (lane < 8)
                else:
                    here = here | ((lane >= start) & (lane < start + 16))
                outer = jnp.where(here, spare, outer)
        one = jnp.where(nearest, outer, zero)
        two = jnp.where(rights, pltpu.roll(outer, LANES - 4, 1), pltpu.roll(outer, 4, 1))
        e_ref[h, pl.ds(0, 8), :] = jnp.where(unused, zero, one)
        e_ref[h, pl.ds(BROAD - 8, 8), :] = jnp.where(unused | ~nearest, zero, two)
        return carry

    lax.fori_loop(0, HIGH, unfold, 0, unroll=4)

    def pair(out_ref, i, near, far):
        right, n, mask = beside_lanes(i)
        for j in range(COLS):
            a, b = e_ref[near, pl.ds(8 * j, 8), :], e_ref[far, pl.ds(8 * j, 8), :]
            moved = jnp.where(right, pltpu.roll(b, n, 1), pltpu.roll(b, LANES - n, 1))
            out_ref[i, pl.ds(8 * j, 8), :] = jnp.where(mask, a, moved)

    def both(i, carry):
        pair(low_ref, i, i, HIGH - 1 - i)
        pair(top_ref, i, HIGH - 1 - i, i)
        return carry

    lax.fori_loop(0, HALF, both, 0, unroll=2)


def fill(refs, temp, at):
    lane = lane_ids()
    zero = jnp.float32(0.0)
    fringe = ((lane >= 64) & (lane < 72)) | (lane >= 120)
    for j in range(COLS):
        edge = temp[3, pl.ds(j, 8, stride=COLS), :]
        for a, ref in enumerate(refs):
            main = temp[a, pl.ds(j, 8, stride=COLS), :]
            for parity in range(2):
                turn = 8 * (2 * a + parity)
                near = pltpu.roll(edge, LANES - turn, 1) if turn else edge
                near = jnp.where(fringe, near, zero)
                mid = pltpu.roll(main, 64, 1) if parity else main
                ref[parity, at, j] = jnp.where(lane < 64, mid, near)


def fill_own(refs, temp, s_ref, e_ref, before_ref, after_ref):
    def layer(h, carry):
        for a in range(3):
            temp[a, pl.ds(HALO, WIDE), :] = s_ref[h, a]
            temp[a, pl.ds(0, HALO), :] = before_ref[h, a]
            temp[a, pl.ds(HALO + WIDE, HALO), :] = after_ref[h, a]
        temp[3] = e_ref[h]
        fill(refs, temp, h)
        return carry

    lax.fori_loop(0, HIGH, layer, 0)


def fill_beside(refs, temp, s_ref, rim_ref, edge_ref, layers):
    def pair(i, carry):
        near, far = layers(i)
        for a in range(3):
            temp[a, pl.ds(0, HALO), :] = rim_ref[i, pl.ds(2 * HALO * a, HALO), :]
            temp[a, pl.ds(HALO, WIDE), :] = s_ref[near % HIGH, a]
            temp[a, pl.ds(HALO + WIDE, HALO), :] = rim_ref[i, pl.ds(2 * HALO * a + HALO, HALO), :]
        temp[3] = edge_ref[i]
        fill(refs, temp, near)
        for a in range(3):
            before = rim_ref[i, pl.ds(2 * HALO * a, HALO), :]
            temp[a, pl.ds(0, HALO), :] = pltpu.roll(before, (HALO - i) % HALO, 0)
            temp[a, pl.ds(HALO, WIDE), :] = s_ref[far % HIGH, a]
            after = rim_ref[i, pl.ds(2 * HALO * a + HALO, HALO), :]
            temp[a, pl.ds(HALO + WIDE, HALO), :] = pltpu.roll(after, i, 0)
        right, n, _ = beside_lanes(i)
        k = lane_ids() % 8
        mask = (right & (k < 8 - n)) | (~right & (k >= n))
        for j in range(COLS):
            both = edge_ref[i, pl.ds(8 * j, 8), :]
            moved = jnp.where(right, pltpu.roll(both, LANES - n, 1), pltpu.roll(both, n, 1))
            temp[3, pl.ds(8 * j, 8), :] = jnp.where(mask, moved, jnp.float32(0.0))
        fill(refs, temp, far)
        return carry

    lax.fori_loop(0, HALF, pair, 0)


def corner():
    return (
        lax.axis_index("hgt") * HIGH - HALO,
        lax.axis_index("wid") * WIDE - HALO,
        lax.axis_index("len") * DEEP,
    )


def list_receivers(rec_ref, todo):
    start = corner()

    def note(r, count):
        h = rec_ref[0, r] - start[0]
        w = rec_ref[1, r] - start[1]
        d = rec_ref[2, r] - start[2]
        mine = (h >= HALO) & (h < HALO + HIGH) & (w >= HALO) & (w < HALO + WIDE)
        mine = mine & (d >= 0) & (d < DEEP)

        @pl.when(mine)
        def _():
            todo[0, count] = r
            todo[1, count] = h
            todo[2, count] = w % COLS
            todo[3, count] = w // COLS
            todo[4, count] = d % 2
            todo[5, count] = d // 2

        return count + mine.astype(jnp.int32)

    todo[6, 0] = lax.fori_loop(0, rec_ref.shape[1], note, jnp.int32(0), unroll=8)


def list_sources(src_ref):
    lane = lane_ids()
    row = lax.broadcasted_iota(jnp.int32, (8, LANES), 0)
    start = corner()
    points = []
    for s in range(src_ref.shape[0]):
        h = src_ref[s, 0] - start[0]
        w = src_ref[s, 1] - start[1]
        d = src_ref[s, 2] - start[2] + HALO
        near = (h >= 0) & (h < TALL) & (w >= 0) & (w < BROAD) & (d >= 0) & (d < DEEP + 2 * HALO)
        h = jnp.clip(h, 0, TALL - 1)
        w = jnp.clip(w, 0, BROAD - 1)
        d = jnp.clip(d, 0, DEEP + 2 * HALO - 1)
        place = (d // 2 + LANES - HALO // 2) % LANES
        points.append((near, d % 2, h, w % COLS, (row == w // COLS) & (lane == place)))
    return points


def sweep(now, old, p_ref, first, trips, layers):
    def chunk(i, carry):
        for u in range(layers):
            h = first(i) + u
            for part in range(2):
                js = range(part * COLS // 2, (part + 1) * COLS // 2)
                for parity in range(2):
                    side = {j: now[1 - parity, h, j] for j in js}
                    rolled = {j: pltpu.roll(side[j], 127 if parity else 1, 1) for j in js}
                    near = range(max(js[0] - 1, 0), min(js[-1] + 2, COLS))
                    mine = {j: now[parity, h, j] for j in near}
                    if part == 0:
                        mine[-1] = pltpu.roll(now[parity, h, COLS - 1], 1, 0)
                    else:
                        mine[COLS] = pltpu.roll(now[parity, h, 0], 7, 0)
                    known = {}
                    for j in js:
                        past = old[parity, h, j]
                        total = now[parity, h - 1, j] + now[parity, h + 1, j]
                        total = total + (mine[j - 1] + mine[j + 1]) + side[j]
                        known[j] = (past, total - 6.0 * past)
                    for j in js:
                        past, total = known[j]
                        old[parity, h, j] = past + p_ref[parity, h, j] * (total + rolled[j])
        return carry

    lax.fori_loop(0, trips, chunk, 0)


def inject(field, points, sig_ref, t, base, inside):
    for s, (near, parity, h, j, spot) in enumerate(points):

        @pl.when(near & inside(h))
        def _():
            add = jnp.where(spot, sig_ref[s, t], jnp.float32(0.0))
            field[parity, h - base, j] = field[parity, h - base, j] + add


def keep(field, todo, hist, t, base):
    def one(i, carry):
        row = field[todo[4, i], todo[1, i] - base, todo[2, i], pl.ds(todo[3, i], 1), :]
        hist[i, pl.ds(t, 1), :] = row
        return carry

    lax.fori_loop(0, todo[6, 0], one, 0)


def gather(trace, todo, hist, early):
    lane = lax.broadcasted_iota(jnp.int32, (STEPS, LANES), 1)
    step = lax.broadcasted_iota(jnp.int32, (STEPS, LANES), 0)

    def one(i, carry):
        number, h = todo[0, i], todo[1, i]
        moved = pltpu.roll(hist[i], (number - todo[5, i] + LANES) % LANES, 1)
        done_early = (h > HALO + step) & (h < TALL - HALO - 1 - step)
        now = done_early if early else ~done_early
        trace[...] = jnp.where((lane == number) & now, moved, trace[...])
        return carry

    lax.fori_loop(0, todo[6, 0], one, 0)


def inner_kernel(src_ref, sig_ref, todo, *refs):
    a_ref, b_ref, p_ref, trace_ref, temp, hist = refs[4:]
    fill_own((a_ref, b_ref, p_ref), temp, *refs[:4])
    points = list_sources(src_ref)

    def step(now, old, t):
        sweep(now, old, p_ref, lambda i: t + 1 + 2 * i, HALF - 1 - t, 2)
        inject(old, points, sig_ref, t, HALO, lambda h: (h > HALO + t) & (h < HALO + HIGH - 1 - t))
        keep(old, todo, hist, t, HALO)

    def pair(i, carry):
        step(a_ref, b_ref, 2 * i)
        step(b_ref, a_ref, 2 * i + 1)
        return carry

    lax.fori_loop(0, HALF // 2, pair, 0)
    trace_ref[...] = jnp.zeros((STEPS, LANES), jnp.float32)
    gather(trace_ref, todo, hist, True)


def march_kernel(src_ref, sig_ref, todo, *refs):
    own = refs[:3]
    early_ref, under, over = refs[3], refs[4:7], refs[7:10]
    out_ref, trace_ref = refs[10:12]
    a_ref, b_ref, p_ref, temp, hist = refs[12:]
    fields = (a_ref, b_ref, p_ref)

    def take(h, carry):
        for ref, got in zip(fields, own):
            for parity in range(2):
                ref[parity, HALO + h] = got[parity, h]
        return carry

    lax.fori_loop(0, HIGH, take, 0)
    fill_beside(fields, temp, *under, lambda i: (HALO - 1 - i, i))
    fill_beside(fields, temp, *over, lambda i: (HALO + HIGH + i, TALL - 1 - i))
    points = list_sources(src_ref)

    def step(now, old, t):
        early = t < HALF - 1
        full = TALL - 2 * (t + 1)
        fours = jnp.where(early, HIGH // 2, full // 4)
        gap = jnp.where(early, HIGH - 2 * (t + 1), 0)
        sweep(
            now,
            old,
            p_ref,
            lambda i: t + 1 + 4 * i + jnp.where(i >= HIGH // 4, gap, 0),
            fours,
            4,
        )
        sweep(now, old, p_ref, lambda i: t + 1 + 4 * fours, jnp.where(early, 0, (full % 4) // 2), 2)
        inject(old, points, sig_ref, t, 0, lambda h: (h <= HALO + t) | (h >= HALO + HIGH - 1 - t))
        keep(old, todo, hist, t, 0)

    def pair(i, carry):
        step(a_ref, b_ref, 2 * i)
        step(b_ref, a_ref, 2 * i + 1)
        return carry

    lax.fori_loop(0, STEPS // 2, pair, 0)

    trace_ref[0] = early_ref[...]
    gather(trace_ref.at[0], todo, hist, False)
    for i in range(1, trace_ref.shape[0]):
        trace_ref[i] = trace_ref[0]

    lane = lane_ids()
    plain = temp.at[0]

    def hand_on(h, carry):
        for j in range(COLS):
            even, odd = a_ref[0, HALO + h, j], a_ref[1, HALO + h, j]
            joined = jnp.where(lane < 64, even, pltpu.roll(odd, 64, 1))
            plain[pl.ds(j, 8, stride=COLS), :] = joined
        out_ref[h] = plain[pl.ds(HALO, WIDE), :]
        return carry

    lax.fori_loop(0, HIGH, hand_on, 0, unroll=4)


def order_kernel(split_ref, out_ref):
    order = in_order()

    def layer(h, carry):
        for j in range(WIDE // 8):
            rows = pl.ds(8 * j, 8)
            out_ref[h, rows, :] = regroup(split_ref[h, rows, :], order)
        return carry

    lax.fori_loop(0, split_ref.shape[0], layer, 0)


def relay_kernel(got_ref, out_ref):
    total = got_ref[0]
    for i in range(1, got_ref.shape[0]):
        total = total + got_ref[i]
    for i in range(out_ref.shape[0]):
        out_ref[i] = total


def total_kernel(got_ref, out_ref):
    total = got_ref[0]
    for i in range(1, got_ref.shape[0]):
        total = total + got_ref[i]
    out_ref[...] = total


def field(*shape):
    return jax.ShapeDtypeStruct(shape, jnp.float32)


def call(kernel, name, outs, ins, scratch=(), scalars=0, limit=8, listed=False):
    out_shape = [field(*shape) for shape in outs]
    out_specs = [VMEM for _ in outs]
    if listed:
        out_shape.append(jax.ShapeDtypeStruct((8, LANES), jnp.int32))
        out_specs.append(SMEM)
    return pl.pallas_call(
        kernel,
        out_shape=tuple(out_shape),
        in_specs=[SMEM] * scalars + [VMEM] * (len(ins) - scalars),
        out_specs=tuple(out_specs),
        scratch_shapes=list(scratch),
        name=name,
        compiler_params=pltpu.CompilerParams(vmem_limit_bytes=limit << 20),
    )(*ins)


def shift(x, axis, move):
    size = lax.axis_size(axis)
    pairs = [(i, i + move) for i in range(size) if 0 <= i + move < size]
    return lax.ppermute(x, axis, pairs)


def per_device(
    pressure_now, pressure_old, classes, admittance, source_cells, source_signal, receiver_cells
):
    face = (HIGH, 3, HALO, LANES)
    block = (HIGH, WIDE, DEEP)
    s, head, tail = pl.pallas_call(
        pack_kernel,
        out_shape=(field(HIGH, 3, WIDE, LANES), field(*face), field(*face)),
        in_specs=[HBM] * 4,
        out_specs=(HBM,) * 3,
        scratch_shapes=[
            pltpu.SMEM(admittance.shape, jnp.float32),
            pltpu.VMEM(block, jnp.float32),
            pltpu.VMEM(block, jnp.float32),
            pltpu.VMEM(block, jnp.int32),
            pltpu.VMEM((HIGH, 3, WIDE, LANES), jnp.float32),
            pltpu.VMEM(face, jnp.float32),
            pltpu.VMEM(face, jnp.float32),
            pltpu.SemaphoreType.DMA((PARTS, 3)),
            pltpu.SemaphoreType.DMA((PARTS, 3)),
            pltpu.SemaphoreType.DMA,
        ],
        name="pack",
        compiler_params=pltpu.CompilerParams(vmem_limit_bytes=PACK_LIMIT),
    )(admittance, pressure_now, pressure_old, classes)
    over, under = shift(s, "hgt", -1), shift(s, "hgt", 1)
    before, after = shift(tail, "wid", 1), shift(head, "wid", -1)
    strip = (HIGH, (BROAD - HALO) // 2, LANES)
    mine, todo = call(
        own_strip_kernel,
        "own_strip",
        [(HIGH, WIDE, LANES)],
        [receiver_cells.T, s],
        scalars=1,
        listed=True,
    )
    before, after, mine = lax.optimization_barrier((before, after, mine))
    to_left, to_right = call(strip_kernel, "strip", [strip, strip], [mine, before, after])
    from_right = shift(to_left, "len", -1)
    from_left = shift(to_right, "len", 1)
    wide_rim, long_rim = (HALF, 3 * 2 * HALO, LANES), (HALF, BROAD, LANES)
    low, top = call(wide_rim_kernel, "wide_rim", [wide_rim, wide_rim], [before, after])
    over_rim, under_rim = shift(low, "hgt", -1), shift(top, "hgt", 1)
    edge, low, top = call(
        long_rim_kernel,
        "long_rim",
        [(HIGH, BROAD, LANES), long_rim, long_rim],
        [from_right, from_left],
    )
    over_edge, under_edge = shift(low, "hgt", -1), shift(top, "hgt", 1)
    own = (2, HIGH, COLS, 8, LANES)
    temp = pltpu.VMEM((4, BROAD, LANES), jnp.float32)
    hist = pltpu.VMEM((LANES, STEPS, LANES), jnp.float32)
    now, old, gain, early = call(
        inner_kernel,
        "inner",
        [own, own, own, (STEPS, LANES)],
        [source_cells, source_signal.T, todo]
        + [s, edge, before, after],
        scratch=[temp, hist],
        scalars=3,
        limit=8,
    )
    state = pltpu.VMEM((2, TALL, COLS, 8, LANES), jnp.float32)
    depth = lax.axis_size("len")
    sides = lax.axis_size("wid") * lax.axis_size("hgt")
    split, traces = call(
        march_kernel,
        "march",
        [(HIGH, WIDE, LANES), (depth, STEPS, LANES)],
        [source_cells, source_signal.T, todo, now, old, gain, early]
        + [under, under_rim, under_edge, over, over_rim, over_edge],
        scratch=[state, state, state, temp, hist],
        scalars=3,
        limit=20,
    )
    traces = lax.all_to_all(traces, "len", 0, 0, tiled=True)
    (traces,) = call(relay_kernel, "relay", [(sides, STEPS, LANES)], [traces])
    traces = lax.all_to_all(traces, ("wid", "hgt"), 0, 0, tiled=True)
    (now,) = call(order_kernel, "order", [(HIGH, WIDE, DEEP)], [split])
    (traces,) = call(total_kernel, "total", [(STEPS, LANES)], [traces])
    return now, traces


def solution(mesh):
    block = P("hgt", "wid", "len")
    return jax.shard_map(
        per_device,
        mesh=mesh,
        in_specs=(block, block, block, P(), P(), P(), P()),
        out_specs=(block, P()),
        check_vma=False,
    )
```

```python
import functools

import jax
import jax.numpy as jnp
from jax import lax
from jax.experimental import pallas as pl
from jax.experimental.pallas import tpu as pltpu
from jax.sharding import PartitionSpec as P

STEPS = 16
HALO = 16
LANES = 128
HIGH, WIDE, DEEP = 16, 64, 128
HALF = HIGH // 2
TALL = HIGH + 2 * HALO
BROAD = WIDE + 2 * HALO
COLS = BROAD // 8
VMEM = pl.BlockSpec(memory_space=pltpu.VMEM)
SMEM = pl.BlockSpec(memory_space=pltpu.SMEM)
HBM = pl.BlockSpec(memory_space=pltpu.HBM)
PARTS = 8
PACK_LIMIT = 60 << 20


def lane_ids():
    return lax.broadcasted_iota(jnp.int32, (8, LANES), 1)


def regroup(rows, order):
    return jnp.take_along_axis(rows, order, axis=1, mode="promise_in_bounds")


def even_odd():
    lane = lane_ids()
    return jnp.where(lane < 64, 2 * lane, 2 * lane - 127)


def in_order():
    lane = lane_ids()
    return (lane // 2) + 64 * (lane % 2)


def pack_kernel(
    adm_hbm, now_hbm, old_hbm, cls_hbm, s_hbm, head_hbm, tail_hbm,
    adm_ref, now_ref, old_ref, cls_ref, s_ref, head_ref, tail_ref, sems, out_sems, one_sem
):
    order = even_odd()

    def layer(h, carry):
        for j in range(WIDE // 8):
            rows = pl.ds(8 * j, 8)
            kinds = cls_ref[h, rows, :]
            loss = jnp.zeros((8, LANES), jnp.float32)
            for index in range(adm_ref.shape[0]):
                loss = jnp.where(kinds == index + 1, adm_ref[index], loss)
            gain = jnp.float32(1.0 / 3.0) / (1.0 + loss)
            for a, field in enumerate((now_ref[h, rows, :], old_ref[h, rows, :], gain)):
                split = regroup(field, order)
                s_ref[h, a, rows, :] = split
                if j < HALO // 8:
                    head_ref[h, a, rows, :] = split
                if j >= (WIDE - HALO) // 8:
                    tail_ref[h, a, pl.ds(8 * j - WIDE + HALO, 8), :] = split
        return carry

    layers = HIGH // PARTS
    fields = ((cls_hbm, cls_ref), (now_hbm, now_ref), (old_hbm, old_ref))
    single = pltpu.make_async_copy(adm_hbm, adm_ref, one_sem)
    single.start()
    copies = []
    for part in range(PARTS):
        at = pl.ds(part * layers, layers)
        for n, (src, dst) in enumerate(fields):
            copy = pltpu.make_async_copy(src.at[at], dst.at[at], sems.at[part, n])
            copy.start()
            copies.append(copy)
    results = ((s_ref, s_hbm), (head_ref, head_hbm), (tail_ref, tail_hbm))
    last = []
    single.wait()
    for part in range(PARTS):
        for copy in copies[3 * part : 3 * part + 3]:
            copy.wait()
        lax.fori_loop(part * layers, (part + 1) * layers, layer, 0)
        at = pl.ds(part * layers, layers)
        for n, (src, dst) in enumerate(results):
            copy = pltpu.make_async_copy(src.at[at], dst.at[at], out_sems.at[part, n])
            copy.start()
            last.append(copy)
    for copy in last:
        copy.wait()


def face_lanes(fields):
    lane = lane_ids()
    out = None
    for a, split in enumerate(fields):
        moved = pltpu.roll(split, 72, 1)
        both = jnp.where((lane < 8) | ((lane >= 56) & (lane < 64)), split, moved)
        if a == 0:
            out = both
        else:
            both = pltpu.roll(both, 16 * a, 1)
            here = (lane >= 16 * a) & (lane < 16 * a + 16)
            here = here | ((lane >= 56 + 16 * a) & (lane < 72 + 16 * a))
            out = jnp.where(here, both, out)
    return out


def own_strip_kernel(rec_ref, s_ref, strip_ref, todo):
    list_receivers(rec_ref, todo)

    def layer(h, carry):
        for j in range(WIDE // 8):
            rows = pl.ds(8 * j, 8)
            strip_ref[h, rows, :] = face_lanes([s_ref[h, a, rows, :] for a in range(3)])
        return carry

    lax.fori_loop(0, HIGH, layer, 0, unroll=4)


def strip_kernel(strip_ref, before_ref, after_ref, left_ref, right_ref):
    lane = lane_ids()
    k = lane % 8
    inner = HALO // 2
    rim = face_lanes

    def layer(h, carry):
        low, high = pl.ds(0, inner), pl.ds(inner, inner)
        rims = [rim([before_ref[h, a, high, :] for a in range(3)])]
        for j in range(WIDE // 8):
            rims.append(strip_ref[h, pl.ds(8 * j, 8), :])
        rims.append(rim([after_ref[h, a, low, :] for a in range(3)]))
        one = rim([before_ref[h, a, low, :] for a in range(3)])
        two = rim([after_ref[h, a, high, :] for a in range(3)])
        heads = jnp.where(k < 4, one, pltpu.roll(two, 4, 1))
        tails = jnp.where(k >= 4, one, pltpu.roll(two, LANES - 4, 1))
        outer = jnp.where(lane < 48, heads, tails)
        half = len(rims) // 2
        for j in range(half):
            rows = pl.ds(8 * j, 8)
            other = pltpu.roll(rims[j + half], 64, 1)
            left = jnp.where(lane < 56, rims[j], other)
            right = jnp.where((lane >= 56) & (lane < 104), rims[j], other)
            if j < 3:
                spare = pltpu.roll(outer, 48 - 16 * j, 1)
                left = jnp.where((lane >= 48) & (lane < 64), spare, left)
                right = jnp.where((lane >= 104) & (lane < 120), spare, right)
            left_ref[h, rows, :] = left
            right_ref[h, rows, :] = right
        return carry

    lax.fori_loop(0, HIGH, layer, 0, unroll=4)


def beside_lanes(i):
    lane = lane_ids()
    k = lane % 8
    n = (HALO - i) // 2
    right = (lane >= 64) & (lane < 112)
    return right, n, (right & (k < n)) | (~right & (k >= 8 - n))


def wide_rim_kernel(before_ref, after_ref, low_ref, top_ref):
    row = lax.broadcasted_iota(jnp.int32, (HALO, LANES), 0)

    def pair(out_ref, i, near, far):
        for a in range(3):
            at = 2 * HALO * a
            kept = jnp.where(row > i, before_ref[near, a], pltpu.roll(before_ref[far, a], i, 0))
            out_ref[i, pl.ds(at, HALO), :] = kept
            moved = pltpu.roll(after_ref[far, a], (HALO - i) % HALO, 0)
            kept = jnp.where(row < HALO - i - 1, after_ref[near, a], moved)
            out_ref[i, pl.ds(at + HALO, HALO), :] = kept

    def both(i, carry):
        pair(low_ref, i, i, HIGH - 1 - i)
        pair(top_ref, i, HIGH - 1 - i, i)
        return carry

    lax.fori_loop(0, HALF, both, 0)


def long_rim_kernel(from_right_ref, from_left_ref, e_ref, low_ref, top_ref):
    lane = lane_ids()
    zero = jnp.float32(0.0)
    unused = ((lane >= 40) & (lane < 64)) | ((lane >= 112) & (lane < 120))

    rights = (lane >= 64) & (lane < 112)
    k = lane % 8
    nearest = (rights & (k < 4)) | (~rights & (k >= 4))

    def unfold(h, carry):
        half = (BROAD - HALO) // 16
        outer = zero
        for j in range(half):
            a, b = from_right_ref[h, pl.ds(8 * j, 8), :], from_left_ref[h, pl.ds(8 * j, 8), :]
            first = pltpu.roll(jnp.where(lane < 48, a, b), 64, 1)
            second = jnp.where(rights, a, b)
            at = HALO // 2 + 8 * j
            e_ref[h, pl.ds(at, 8), :] = jnp.where(unused, zero, first)
            e_ref[h, pl.ds(at + 8 * half, 8), :] = jnp.where(unused, zero, second)
            if j < 3:
                spare = pltpu.roll(jnp.where((lane >= 48) & (lane < 64), a, b), 16 + 16 * j, 1)
                here = (lane >= 64 + 16 * j) & (lane < 80 + 16 * j)
                start = (120 + 16 * j) % LANES
                if j == 0:
                    here = here | (lane >= start) | (lane < 8)
                else:
                    here = here | ((lane >= start) & (lane < start + 16))
                outer = jnp.where(here, spare, outer)
        one = jnp.where(nearest, outer, zero)
        two = jnp.where(rights, pltpu.roll(outer, LANES - 4, 1), pltpu.roll(outer, 4, 1))
        e_ref[h, pl.ds(0, 8), :] = jnp.where(unused, zero, one)
        e_ref[h, pl.ds(BROAD - 8, 8), :] = jnp.where(unused | ~nearest, zero, two)
        return carry

    lax.fori_loop(0, HIGH, unfold, 0, unroll=4)

    def pair(out_ref, i, near, far):
        right, n, mask = beside_lanes(i)
        for j in range(COLS):
            a, b = e_ref[near, pl.ds(8 * j, 8), :], e_ref[far, pl.ds(8 * j, 8), :]
            moved = jnp.where(right, pltpu.roll(b, n, 1), pltpu.roll(b, LANES - n, 1))
            out_ref[i, pl.ds(8 * j, 8), :] = jnp.where(mask, a, moved)

    def both(i, carry):
        pair(low_ref, i, i, HIGH - 1 - i)
        pair(top_ref, i, HIGH - 1 - i, i)
        return carry

    lax.fori_loop(0, HALF, both, 0, unroll=2)


def fill(refs, temp, at):
    lane = lane_ids()
    zero = jnp.float32(0.0)
    fringe = ((lane >= 64) & (lane < 72)) | (lane >= 120)
    for j in range(COLS):
        edge = temp[3, pl.ds(j, 8, stride=COLS), :]
        for a, ref in enumerate(refs):
            main = temp[a, pl.ds(j, 8, stride=COLS), :]
            for parity in range(2):
                turn = 8 * (2 * a + parity)
                near = pltpu.roll(edge, LANES - turn, 1) if turn else edge
                near = jnp.where(fringe, near, zero)
                mid = pltpu.roll(main, 64, 1) if parity else main
                ref[parity, at, j] = jnp.where(lane < 64, mid, near)


def fill_own(refs, temp, s_ref, e_ref, before_ref, after_ref):
    def layer(h, carry):
        for a in range(3):
            temp[a, pl.ds(HALO, WIDE), :] = s_ref[h, a]
            temp[a, pl.ds(0, HALO), :] = before_ref[h, a]
            temp[a, pl.ds(HALO + WIDE, HALO), :] = after_ref[h, a]
        temp[3] = e_ref[h]
        fill(refs, temp, h)
        return carry

    lax.fori_loop(0, HIGH, layer, 0)


def fill_main(refs, temp, at):
    lane = lane_ids()
    for j in range(COLS):
        for a, ref in enumerate(refs):
            main = temp[a, pl.ds(j, 8, stride=COLS), :]
            for parity in range(2):
                mid = pltpu.roll(main, 64, 1) if parity else main
                ref[parity, at, j] = jnp.where(lane < 64, mid, jnp.float32(0.0))


def fill_edge(refs, mains, temp, at, source):
    lane = lane_ids()
    fringe = ((lane >= 64) & (lane < 72)) | (lane >= 120)
    for j in range(COLS):
        edge = temp[pl.ds(j, 8, stride=COLS), :]
        for a, (ref, main) in enumerate(zip(refs, mains)):
            for parity in range(2):
                turn = 8 * (2 * a + parity)
                near = pltpu.roll(edge, LANES - turn, 1) if turn else edge
                ref[parity, at, j] = jnp.where(fringe, near, main[parity, source, j])


def fill_beside(refs, temp, s_ref, rim_ref, layers):
    def pair(i, carry):
        near, far = layers(i)
        for a in range(3):
            before = rim_ref[i, pl.ds(2 * HALO * a, HALO), :]
            after = rim_ref[i, pl.ds(2 * HALO * a + HALO, HALO), :]
            temp[a, pl.ds(0, HALO), :] = before
            temp[a, pl.ds(HALO, WIDE), :] = s_ref[near % HIGH, a]
            temp[a, pl.ds(HALO + WIDE, HALO), :] = after
        fill_main(refs, temp, near)
        for a in range(3):
            before = rim_ref[i, pl.ds(2 * HALO * a, HALO), :]
            after = rim_ref[i, pl.ds(2 * HALO * a + HALO, HALO), :]
            temp[a, pl.ds(0, HALO), :] = pltpu.roll(before, (HALO - i) % HALO, 0)
            temp[a, pl.ds(HALO, WIDE), :] = s_ref[far % HIGH, a]
            temp[a, pl.ds(HALO + WIDE, HALO), :] = pltpu.roll(after, i, 0)
        fill_main(refs, temp, far)
        return carry

    lax.fori_loop(0, HALF, pair, 0)


def beside_kernel(under, under_rim, over, over_rim, *refs):
    fields, temp = refs[:3], refs[3]
    fill_beside(fields, temp, under, under_rim, lambda i: (HALO - 1 - i, i))
    fill_beside(fields, temp, over, over_rim, lambda i: (HALO + i, 2 * HALO - 1 - i))


def fill_edges(refs, mains, temp, edge_ref, layers, skip):
    first, second = temp.at[0], temp.at[1]

    def pair(i, carry):
        near, far = layers(i)
        first[...] = edge_ref[i]
        fill_edge(refs, mains, first, near + skip, near)
        right, n, _ = beside_lanes(i)
        k = lane_ids() % 8
        mask = (right & (k < 8 - n)) | (~right & (k >= n))
        for j in range(COLS):
            both = edge_ref[i, pl.ds(8 * j, 8), :]
            moved = jnp.where(right, pltpu.roll(both, LANES - n, 1), pltpu.roll(both, n, 1))
            second[pl.ds(8 * j, 8), :] = jnp.where(mask, moved, jnp.float32(0.0))
        fill_edge(refs, mains, second, far + skip, far)
        return carry

    lax.fori_loop(0, HALF, pair, 0)


def corner():
    return (
        lax.axis_index("hgt") * HIGH - HALO,
        lax.axis_index("wid") * WIDE - HALO,
        lax.axis_index("len") * DEEP,
    )


def list_receivers(rec_ref, todo):
    start = corner()

    def note(r, count):
        h = rec_ref[0, r] - start[0]
        w = rec_ref[1, r] - start[1]
        d = rec_ref[2, r] - start[2]
        mine = (h >= HALO) & (h < HALO + HIGH) & (w >= HALO) & (w < HALO + WIDE)
        mine = mine & (d >= 0) & (d < DEEP)

        @pl.when(mine)
        def _():
            todo[0, count] = r
            todo[1, count] = h
            todo[2, count] = w % COLS
            todo[3, count] = w // COLS
            todo[4, count] = d % 2
            todo[5, count] = d // 2

        return count + mine.astype(jnp.int32)

    todo[6, 0] = lax.fori_loop(0, rec_ref.shape[1], note, jnp.int32(0), unroll=8)


def list_sources(src_ref):
    lane = lane_ids()
    row = lax.broadcasted_iota(jnp.int32, (8, LANES), 0)
    start = corner()
    points = []
    for s in range(src_ref.shape[0]):
        h = src_ref[s, 0] - start[0]
        w = src_ref[s, 1] - start[1]
        d = src_ref[s, 2] - start[2] + HALO
        near = (h >= 0) & (h < TALL) & (w >= 0) & (w < BROAD) & (d >= 0) & (d < DEEP + 2 * HALO)
        h = jnp.clip(h, 0, TALL - 1)
        w = jnp.clip(w, 0, BROAD - 1)
        d = jnp.clip(d, 0, DEEP + 2 * HALO - 1)
        place = (d // 2 + LANES - HALO // 2) % LANES
        points.append((near, d % 2, h, w % COLS, (row == w // COLS) & (lane == place)))
    return points


def sweep(now, old, p_ref, first, trips, layers):
    def chunk(i, carry):
        for u in range(layers):
            h = first(i) + u
            for part in range(2):
                js = range(part * COLS // 2, (part + 1) * COLS // 2)
                for parity in range(2):
                    side = {j: now[1 - parity, h, j] for j in js}
                    rolled = {j: pltpu.roll(side[j], 127 if parity else 1, 1) for j in js}
                    near = range(max(js[0] - 1, 0), min(js[-1] + 2, COLS))
                    mine = {j: now[parity, h, j] for j in near}
                    if part == 0:
                        mine[-1] = pltpu.roll(now[parity, h, COLS - 1], 1, 0)
                    else:
                        mine[COLS] = pltpu.roll(now[parity, h, 0], 7, 0)
                    known = {}
                    for j in js:
                        past = old[parity, h, j]
                        total = now[parity, h - 1, j] + now[parity, h + 1, j]
                        total = total + (mine[j - 1] + mine[j + 1]) + side[j]
                        known[j] = (past, total - 6.0 * past)
                    for j in js:
                        past, total = known[j]
                        old[parity, h, j] = past + p_ref[parity, h, j] * (total + rolled[j])
        return carry

    lax.fori_loop(0, trips, chunk, 0)


def inject(field, points, sig_ref, t, base, inside):
    some = points[0][0]
    for point in points[1:]:
        some = some | point[0]

    @pl.when(some)
    def _():
        for s, (near, parity, h, j, spot) in enumerate(points):

            @pl.when(near & inside(h))
            def _():
                add = jnp.where(spot, sig_ref[s, t], jnp.float32(0.0))
                field[parity, h - base, j] = field[parity, h - base, j] + add


def keep(field, todo, hist, t, base):
    def one(i, carry):
        row = field[todo[4, i], todo[1, i] - base, todo[2, i], pl.ds(todo[3, i], 1), :]
        hist[i, pl.ds(t, 1), :] = row
        return carry

    lax.fori_loop(0, todo[6, 0], one, 0)


def gather(trace, todo, hist, early):
    lane = lax.broadcasted_iota(jnp.int32, (STEPS, LANES), 1)
    step = lax.broadcasted_iota(jnp.int32, (STEPS, LANES), 0)

    def one(i, carry):
        number, h = todo[0, i], todo[1, i]
        moved = pltpu.roll(hist[i], (number - todo[5, i] + LANES) % LANES, 1)
        done_early = (h > HALO + step) & (h < TALL - HALO - 1 - step)
        now = done_early if early else ~done_early
        trace[...] = jnp.where((lane == number) & now, moved, trace[...])
        return carry

    lax.fori_loop(0, todo[6, 0], one, 0)


def inner_kernel(src_ref, sig_ref, todo, *refs):
    a_ref, b_ref, p_ref, trace_ref, temp, hist = refs[4:]
    fill_own((a_ref, b_ref, p_ref), temp, *refs[:4])
    points = list_sources(src_ref)

    def step(now, old, t):
        sweep(now, old, p_ref, lambda i: t + 1 + 2 * i, HALF - 1 - t, 2)
        inject(old, points, sig_ref, t, HALO, lambda h: (h > HALO + t) & (h < HALO + HIGH - 1 - t))
        keep(old, todo, hist, t, HALO)

    def pair(i, carry):
        step(a_ref, b_ref, 2 * i)
        step(b_ref, a_ref, 2 * i + 1)
        return carry

    lax.fori_loop(0, HALF // 2, pair, 0)
    trace_ref[...] = jnp.zeros((STEPS, LANES), jnp.float32)
    gather(trace_ref, todo, hist, True)


def march_kernel(src_ref, sig_ref, todo, *refs):
    own = refs[:3]
    early_ref, mains, under_edge, over_edge = refs[3], refs[4:7], refs[7], refs[8]
    out_ref, trace_ref = refs[9:11]
    a_ref, b_ref, p_ref, temp, hist = refs[11:]
    fields = (a_ref, b_ref, p_ref)

    def take(h, carry):
        for ref, got in zip(fields, own):
            for parity in range(2):
                ref[parity, HALO + h] = got[parity, h]
        return carry

    lax.fori_loop(0, HIGH, take, 0)
    fill_edges(fields, mains, temp, under_edge, lambda i: (HALO - 1 - i, i), 0)
    fill_edges(fields, mains, temp, over_edge, lambda i: (HALO + i, 2 * HALO - 1 - i), HIGH)
    points = list_sources(src_ref)

    def step(now, old, t):
        early = t < HALF - 1
        full = TALL - 2 * (t + 1)
        fours = jnp.where(early, HIGH // 2, full // 4)
        gap = jnp.where(early, HIGH - 2 * (t + 1), 0)
        sweep(
            now,
            old,
            p_ref,
            lambda i: t + 1 + 4 * i + jnp.where(i >= HIGH // 4, gap, 0),
            fours,
            4,
        )
        sweep(now, old, p_ref, lambda i: t + 1 + 4 * fours, jnp.where(early, 0, (full % 4) // 2), 2)
        inject(old, points, sig_ref, t, 0, lambda h: (h <= HALO + t) | (h >= HALO + HIGH - 1 - t))
        keep(old, todo, hist, t, 0)

    def pair(i, carry):
        step(a_ref, b_ref, 2 * i)
        step(b_ref, a_ref, 2 * i + 1)
        return carry

    lax.fori_loop(0, STEPS // 2, pair, 0)

    trace_ref[0] = early_ref[...]
    gather(trace_ref.at[0], todo, hist, False)
    for i in range(1, trace_ref.shape[0]):
        trace_ref[i] = trace_ref[0]

    lane = lane_ids()
    plain = temp.at[0]

    def hand_on(h, carry):
        for j in range(COLS):
            even, odd = a_ref[0, HALO + h, j], a_ref[1, HALO + h, j]
            joined = jnp.where(lane < 64, even, pltpu.roll(odd, 64, 1))
            plain[pl.ds(j, 8, stride=COLS), :] = joined
        out_ref[h] = plain[pl.ds(HALO, WIDE), :]
        return carry

    lax.fori_loop(0, HIGH, hand_on, 0, unroll=4)


def order_kernel(split_ref, out_ref):
    order = in_order()

    def layer(h, carry):
        for j in range(WIDE // 8):
            rows = pl.ds(8 * j, 8)
            out_ref[h, rows, :] = regroup(split_ref[h, rows, :], order)
        return carry

    lax.fori_loop(0, split_ref.shape[0], layer, 0)


def relay_kernel(got_ref, out_ref):
    total = got_ref[0]
    for i in range(1, got_ref.shape[0]):
        total = total + got_ref[i]
    for i in range(out_ref.shape[0]):
        out_ref[i] = total


def total_kernel(got_ref, out_ref):
    total = got_ref[0]
    for i in range(1, got_ref.shape[0]):
        total = total + got_ref[i]
    out_ref[...] = total


def field(*shape):
    return jax.ShapeDtypeStruct(shape, jnp.float32)


def call(kernel, name, outs, ins, scratch=(), scalars=0, limit=8, listed=False):
    out_shape = [field(*shape) for shape in outs]
    out_specs = [VMEM for _ in outs]
    if listed:
        out_shape.append(jax.ShapeDtypeStruct((8, LANES), jnp.int32))
        out_specs.append(SMEM)
    return pl.pallas_call(
        kernel,
        out_shape=tuple(out_shape),
        in_specs=[SMEM] * scalars + [VMEM] * (len(ins) - scalars),
        out_specs=tuple(out_specs),
        scratch_shapes=list(scratch),
        name=name,
        compiler_params=pltpu.CompilerParams(vmem_limit_bytes=limit << 20),
    )(*ins)


def shift(x, axis, move):
    size = lax.axis_size(axis)
    pairs = [(i, i + move) for i in range(size) if 0 <= i + move < size]
    return lax.ppermute(x, axis, pairs)


def per_device(
    pressure_now, pressure_old, classes, admittance, source_cells, source_signal, receiver_cells
):
    face = (HIGH, 3, HALO, LANES)
    block = (HIGH, WIDE, DEEP)
    s, head, tail = pl.pallas_call(
        pack_kernel,
        out_shape=(field(HIGH, 3, WIDE, LANES), field(*face), field(*face)),
        in_specs=[HBM] * 4,
        out_specs=(HBM,) * 3,
        scratch_shapes=[
            pltpu.SMEM(admittance.shape, jnp.float32),
            pltpu.VMEM(block, jnp.float32),
            pltpu.VMEM(block, jnp.float32),
            pltpu.VMEM(block, jnp.int32),
            pltpu.VMEM((HIGH, 3, WIDE, LANES), jnp.float32),
            pltpu.VMEM(face, jnp.float32),
            pltpu.VMEM(face, jnp.float32),
            pltpu.SemaphoreType.DMA((PARTS, 3)),
            pltpu.SemaphoreType.DMA((PARTS, 3)),
            pltpu.SemaphoreType.DMA,
        ],
        name="pack",
        compiler_params=pltpu.CompilerParams(vmem_limit_bytes=PACK_LIMIT),
    )(admittance, pressure_now, pressure_old, classes)
    over, under = shift(s, "hgt", -1), shift(s, "hgt", 1)
    before, after = shift(tail, "wid", 1), shift(head, "wid", -1)
    strip = (HIGH, (BROAD - HALO) // 2, LANES)
    mine, todo = call(
        own_strip_kernel,
        "own_strip",
        [(HIGH, WIDE, LANES)],
        [receiver_cells.T, s],
        scalars=1,
        listed=True,
    )
    before, after, mine = lax.optimization_barrier((before, after, mine))
    to_left, to_right = call(strip_kernel, "strip", [strip, strip], [mine, before, after])
    from_right = shift(to_left, "len", -1)
    from_left = shift(to_right, "len", 1)
    wide_rim, long_rim = (HALF, 3 * 2 * HALO, LANES), (HALF, BROAD, LANES)
    low, top = call(wide_rim_kernel, "wide_rim", [wide_rim, wide_rim], [before, after])
    over_rim, under_rim = shift(low, "hgt", -1), shift(top, "hgt", 1)
    edge, low, top = call(
        long_rim_kernel,
        "long_rim",
        [(HIGH, BROAD, LANES), long_rim, long_rim],
        [from_right, from_left],
    )
    under_edge = shift(top, "hgt", 1)
    low, under = lax.optimization_barrier((low, under))
    over_edge = shift(low, "hgt", -1)
    own = (2, HIGH, COLS, 8, LANES)
    temp = pltpu.VMEM((4, BROAD, LANES), jnp.float32)
    hist = pltpu.VMEM((LANES, STEPS, LANES), jnp.float32)
    now, old, gain, early = call(
        inner_kernel,
        "inner",
        [own, own, own, (STEPS, LANES)],
        [source_cells, source_signal.T, todo]
        + [s, edge, before, after],
        scratch=[temp, hist],
        scalars=3,
        limit=8,
    )
    halos = (2, 2 * HALO, COLS, 8, LANES)
    mains = call(
        beside_kernel,
        "beside",
        [halos] * 3,
        [under, under_rim, over, over_rim],
        scratch=[temp],
        limit=16,
    )
    state = pltpu.VMEM((2, TALL, COLS, 8, LANES), jnp.float32)
    depth = lax.axis_size("len")
    sides = lax.axis_size("wid") * lax.axis_size("hgt")
    split, traces = call(
        march_kernel,
        "march",
        [(HIGH, WIDE, LANES), (depth, STEPS, LANES)],
        [source_cells, source_signal.T, todo, now, old, gain, early]
        + [*mains, under_edge, over_edge],
        scratch=[state, state, state, temp, hist],
        scalars=3,
        limit=20,
    )
    traces = lax.all_to_all(traces, "len", 0, 0, tiled=True)
    (traces,) = call(relay_kernel, "relay", [(sides, STEPS, LANES)], [traces])
    traces = lax.all_to_all(traces, ("wid", "hgt"), 0, 0, tiled=True)
    (now,) = call(order_kernel, "order", [(HIGH, WIDE, DEEP)], [split])
    (traces,) = call(total_kernel, "total", [(STEPS, LANES)], [traces])
    return now, traces


def solution(mesh):
    block = P("hgt", "wid", "len")
    return jax.shard_map(
        per_device,
        mesh=mesh,
        in_specs=(block, block, block, P(), P(), P(), P()),
        out_specs=(block, P()),
        check_vma=False,
    )
```

```python
import functools

import jax
import jax.numpy as jnp
from jax import lax
from jax.experimental import pallas as pl
from jax.experimental.pallas import tpu as pltpu
from jax.sharding import PartitionSpec as P

STEPS = 16
HALO = 16
LANES = 128
HIGH, WIDE, DEEP = 16, 64, 128
HALF = HIGH // 2
TALL = HIGH + 2 * HALO
BROAD = WIDE + 2 * HALO
COLS = BROAD // 8
VMEM = pl.BlockSpec(memory_space=pltpu.VMEM)
SMEM = pl.BlockSpec(memory_space=pltpu.SMEM)
HBM = pl.BlockSpec(memory_space=pltpu.HBM)
PARTS = 8
PACK_LIMIT = 60 << 20


def lane_ids():
    return lax.broadcasted_iota(jnp.int32, (8, LANES), 1)


def regroup(rows, order):
    return jnp.take_along_axis(rows, order, axis=1, mode="promise_in_bounds")


def even_odd():
    lane = lane_ids()
    return jnp.where(lane < 64, 2 * lane, 2 * lane - 127)


def in_order():
    lane = lane_ids()
    return (lane // 2) + 64 * (lane % 2)


def pack_kernel(
    adm_hbm, now_hbm, old_hbm, cls_hbm, s_hbm, head_hbm, tail_hbm,
    adm_ref, now_ref, old_ref, cls_ref, s_ref, head_ref, tail_ref, sems, out_sems, one_sem
):
    order = even_odd()

    def layer(h, carry):
        for j in range(WIDE // 8):
            rows = pl.ds(8 * j, 8)
            kinds = cls_ref[h, rows, :]
            loss = jnp.zeros((8, LANES), jnp.float32)
            for index in range(adm_ref.shape[0]):
                loss = jnp.where(kinds == index + 1, adm_ref[index], loss)
            gain = jnp.float32(1.0 / 3.0) / (1.0 + loss)
            for a, field in enumerate((now_ref[h, rows, :], old_ref[h, rows, :], gain)):
                split = regroup(field, order)
                s_ref[h, a, rows, :] = split
                if j < HALO // 8:
                    head_ref[h, a, rows, :] = split
                if j >= (WIDE - HALO) // 8:
                    tail_ref[h, a, pl.ds(8 * j - WIDE + HALO, 8), :] = split
        return carry

    layers = HIGH // PARTS
    fields = ((cls_hbm, cls_ref), (now_hbm, now_ref), (old_hbm, old_ref))
    single = pltpu.make_async_copy(adm_hbm, adm_ref, one_sem)
    single.start()
    copies = []
    for part in range(PARTS):
        at = pl.ds(part * layers, layers)
        for n, (src, dst) in enumerate(fields):
            copy = pltpu.make_async_copy(src.at[at], dst.at[at], sems.at[part, n])
            copy.start()
            copies.append(copy)
    results = ((s_ref, s_hbm), (head_ref, head_hbm), (tail_ref, tail_hbm))
    last = []
    single.wait()
    for part in range(PARTS):
        for copy in copies[3 * part : 3 * part + 3]:
            copy.wait()
        lax.fori_loop(part * layers, (part + 1) * layers, layer, 0)
        at = pl.ds(part * layers, layers)
        for n, (src, dst) in enumerate(results):
            copy = pltpu.make_async_copy(src.at[at], dst.at[at], out_sems.at[part, n])
            copy.start()
            last.append(copy)
    for copy in last:
        copy.wait()


def face_lanes(fields):
    lane = lane_ids()
    out = None
    for a, split in enumerate(fields):
        moved = pltpu.roll(split, 72, 1)
        both = jnp.where((lane < 8) | ((lane >= 56) & (lane < 64)), split, moved)
        if a == 0:
            out = both
        else:
            both = pltpu.roll(both, 16 * a, 1)
            here = (lane >= 16 * a) & (lane < 16 * a + 16)
            here = here | ((lane >= 56 + 16 * a) & (lane < 72 + 16 * a))
            out = jnp.where(here, both, out)
    return out


def own_strip_kernel(rec_ref, s_ref, strip_ref, todo):
    list_receivers(rec_ref, todo)

    def layer(h, carry):
        for j in range(WIDE // 8):
            rows = pl.ds(8 * j, 8)
            strip_ref[h, rows, :] = face_lanes([s_ref[h, a, rows, :] for a in range(3)])
        return carry

    lax.fori_loop(0, HIGH, layer, 0, unroll=4)


def strip_kernel(strip_ref, before_ref, after_ref, left_ref, right_ref):
    lane = lane_ids()
    k = lane % 8
    inner = HALO // 2
    rim = face_lanes

    def layer(h, carry):
        low, high = pl.ds(0, inner), pl.ds(inner, inner)
        rims = [rim([before_ref[h, a, high, :] for a in range(3)])]
        for j in range(WIDE // 8):
            rims.append(strip_ref[h, pl.ds(8 * j, 8), :])
        rims.append(rim([after_ref[h, a, low, :] for a in range(3)]))
        one = rim([before_ref[h, a, low, :] for a in range(3)])
        two = rim([after_ref[h, a, high, :] for a in range(3)])
        heads = jnp.where(k < 4, one, pltpu.roll(two, 4, 1))
        tails = jnp.where(k >= 4, one, pltpu.roll(two, LANES - 4, 1))
        outer = jnp.where(lane < 48, heads, tails)
        half = len(rims) // 2
        for j in range(half):
            rows = pl.ds(8 * j, 8)
            other = pltpu.roll(rims[j + half], 64, 1)
            left = jnp.where(lane < 56, rims[j], other)
            right = jnp.where((lane >= 56) & (lane < 104), rims[j], other)
            if j < 3:
                spare = pltpu.roll(outer, 48 - 16 * j, 1)
                left = jnp.where((lane >= 48) & (lane < 64), spare, left)
                right = jnp.where((lane >= 104) & (lane < 120), spare, right)
            left_ref[h, rows, :] = left
            right_ref[h, rows, :] = right
        return carry

    lax.fori_loop(0, HIGH, layer, 0, unroll=4)


def beside_lanes(i):
    lane = lane_ids()
    k = lane % 8
    n = (HALO - i) // 2
    right = (lane >= 64) & (lane < 112)
    return right, n, (right & (k < n)) | (~right & (k >= 8 - n))


def wide_rim_kernel(before_ref, after_ref, low_ref, top_ref):
    row = lax.broadcasted_iota(jnp.int32, (HALO, LANES), 0)

    def pair(out_ref, i, near, far):
        for a in range(3):
            at = 2 * HALO * a
            kept = jnp.where(row > i, before_ref[near, a], pltpu.roll(before_ref[far, a], i, 0))
            out_ref[i, pl.ds(at, HALO), :] = kept
            moved = pltpu.roll(after_ref[far, a], (HALO - i) % HALO, 0)
            kept = jnp.where(row < HALO - i - 1, after_ref[near, a], moved)
            out_ref[i, pl.ds(at + HALO, HALO), :] = kept

    def both(i, carry):
        pair(low_ref, i, i, HIGH - 1 - i)
        pair(top_ref, i, HIGH - 1 - i, i)
        return carry

    lax.fori_loop(0, HALF, both, 0)


def long_rim_kernel(from_right_ref, from_left_ref, e_ref, low_ref, top_ref):
    lane = lane_ids()
    zero = jnp.float32(0.0)
    unused = ((lane >= 40) & (lane < 64)) | ((lane >= 112) & (lane < 120))

    rights = (lane >= 64) & (lane < 112)
    k = lane % 8
    nearest = (rights & (k < 4)) | (~rights & (k >= 4))

    def unfold(h, carry):
        half = (BROAD - HALO) // 16
        outer = zero
        for j in range(half):
            a, b = from_right_ref[h, pl.ds(8 * j, 8), :], from_left_ref[h, pl.ds(8 * j, 8), :]
            first = pltpu.roll(jnp.where(lane < 48, a, b), 64, 1)
            second = jnp.where(rights, a, b)
            at = HALO // 2 + 8 * j
            e_ref[h, pl.ds(at, 8), :] = jnp.where(unused, zero, first)
            e_ref[h, pl.ds(at + 8 * half, 8), :] = jnp.where(unused, zero, second)
            if j < 3:
                spare = pltpu.roll(jnp.where((lane >= 48) & (lane < 64), a, b), 16 + 16 * j, 1)
                here = (lane >= 64 + 16 * j) & (lane < 80 + 16 * j)
                start = (120 + 16 * j) % LANES
                if j == 0:
                    here = here | (lane >= start) | (lane < 8)
                else:
                    here = here | ((lane >= start) & (lane < start + 16))
                outer = jnp.where(here, spare, outer)
        one = jnp.where(nearest, outer, zero)
        two = jnp.where(rights, pltpu.roll(outer, LANES - 4, 1), pltpu.roll(outer, 4, 1))
        e_ref[h, pl.ds(0, 8), :] = jnp.where(unused, zero, one)
        e_ref[h, pl.ds(BROAD - 8, 8), :] = jnp.where(unused | ~nearest, zero, two)
        return carry

    lax.fori_loop(0, HIGH, unfold, 0, unroll=4)

    def pair(out_ref, i, near, far):
        right, n, mask = beside_lanes(i)
        for j in range(COLS):
            a, b = e_ref[near, pl.ds(8 * j, 8), :], e_ref[far, pl.ds(8 * j, 8), :]
            moved = jnp.where(right, pltpu.roll(b, n, 1), pltpu.roll(b, LANES - n, 1))
            out_ref[i, pl.ds(8 * j, 8), :] = jnp.where(mask, a, moved)

    def both(i, carry):
        pair(low_ref, i, i, HIGH - 1 - i)
        pair(top_ref, i, HIGH - 1 - i, i)
        return carry

    lax.fori_loop(0, HALF, both, 0, unroll=2)


def fill(refs, temp, at):
    lane = lane_ids()
    zero = jnp.float32(0.0)
    fringe = ((lane >= 64) & (lane < 72)) | (lane >= 120)
    for j in range(COLS):
        edge = temp[3, pl.ds(j, 8, stride=COLS), :]
        for a, ref in enumerate(refs):
            main = temp[a, pl.ds(j, 8, stride=COLS), :]
            for parity in range(2):
                turn = 8 * (2 * a + parity)
                near = pltpu.roll(edge, LANES - turn, 1) if turn else edge
                near = jnp.where(fringe, near, zero)
                mid = pltpu.roll(main, 64, 1) if parity else main
                ref[parity, at, j] = jnp.where(lane < 64, mid, near)


def fill_own(refs, temp, s_ref, e_ref, before_ref, after_ref):
    def layer(h, carry):
        for a in range(3):
            temp[a, pl.ds(HALO, WIDE), :] = s_ref[h, a]
            temp[a, pl.ds(0, HALO), :] = before_ref[h, a]
            temp[a, pl.ds(HALO + WIDE, HALO), :] = after_ref[h, a]
        temp[3] = e_ref[h]
        fill(refs, temp, h)
        return carry

    lax.fori_loop(0, HIGH, layer, 0)


def fill_main(refs, temp, at):
    lane = lane_ids()
    for j in range(COLS):
        for a, ref in enumerate(refs):
            main = temp[a, pl.ds(j, 8, stride=COLS), :]
            for parity in range(2):
                mid = pltpu.roll(main, 64, 1) if parity else main
                ref[parity, at, j] = jnp.where(lane < 64, mid, jnp.float32(0.0))


def fill_edge(refs, mains, temp, at, source):
    lane = lane_ids()
    fringe = ((lane >= 64) & (lane < 72)) | (lane >= 120)
    for j in range(COLS):
        edge = temp[pl.ds(j, 8, stride=COLS), :]
        for a, (ref, main) in enumerate(zip(refs, mains)):
            for parity in range(2):
                turn = 8 * (2 * a + parity)
                near = pltpu.roll(edge, LANES - turn, 1) if turn else edge
                ref[parity, at, j] = jnp.where(fringe, near, main[parity, source, j])


def fill_beside(refs, temp, s_ref, rim_ref, layers):
    def pair(i, carry):
        near, far = layers(i)
        for a in range(3):
            before = rim_ref[i, pl.ds(2 * HALO * a, HALO), :]
            after = rim_ref[i, pl.ds(2 * HALO * a + HALO, HALO), :]
            temp[a, pl.ds(0, HALO), :] = before
            temp[a, pl.ds(HALO, WIDE), :] = s_ref[near % HIGH, a]
            temp[a, pl.ds(HALO + WIDE, HALO), :] = after
        fill_main(refs, temp, near)
        for a in range(3):
            before = rim_ref[i, pl.ds(2 * HALO * a, HALO), :]
            after = rim_ref[i, pl.ds(2 * HALO * a + HALO, HALO), :]
            temp[a, pl.ds(0, HALO), :] = pltpu.roll(before, (HALO - i) % HALO, 0)
            temp[a, pl.ds(HALO, WIDE), :] = s_ref[far % HIGH, a]
            temp[a, pl.ds(HALO + WIDE, HALO), :] = pltpu.roll(after, i, 0)
        fill_main(refs, temp, far)
        return carry

    lax.fori_loop(0, HALF, pair, 0)


def beside_kernel(under, under_rim, over, over_rim, *refs):
    fields, temp = refs[:3], refs[3]
    fill_beside(fields, temp, under, under_rim, lambda i: (HALO - 1 - i, i))
    fill_beside(fields, temp, over, over_rim, lambda i: (HALO + i, 2 * HALO - 1 - i))


def fill_edges(refs, mains, temp, edge_ref, layers, skip):
    first, second = temp.at[0], temp.at[1]

    def pair(i, carry):
        near, far = layers(i)
        first[...] = edge_ref[i]
        fill_edge(refs, mains, first, near + skip, near)
        right, n, _ = beside_lanes(i)
        k = lane_ids() % 8
        mask = (right & (k < 8 - n)) | (~right & (k >= n))
        for j in range(COLS):
            both = edge_ref[i, pl.ds(8 * j, 8), :]
            moved = jnp.where(right, pltpu.roll(both, LANES - n, 1), pltpu.roll(both, n, 1))
            second[pl.ds(8 * j, 8), :] = jnp.where(mask, moved, jnp.float32(0.0))
        fill_edge(refs, mains, second, far + skip, far)
        return carry

    lax.fori_loop(0, HALF, pair, 0, unroll=2)


def corner():
    return (
        lax.axis_index("hgt") * HIGH - HALO,
        lax.axis_index("wid") * WIDE - HALO,
        lax.axis_index("len") * DEEP,
    )


def list_receivers(rec_ref, todo):
    start = corner()

    def note(r, count):
        h = rec_ref[0, r] - start[0]
        w = rec_ref[1, r] - start[1]
        d = rec_ref[2, r] - start[2]
        mine = (h >= HALO) & (h < HALO + HIGH) & (w >= HALO) & (w < HALO + WIDE)
        mine = mine & (d >= 0) & (d < DEEP)

        @pl.when(mine)
        def _():
            todo[0, count] = r
            todo[1, count] = h
            todo[2, count] = w % COLS
            todo[3, count] = w // COLS
            todo[4, count] = d % 2
            todo[5, count] = d // 2

        return count + mine.astype(jnp.int32)

    todo[6, 0] = lax.fori_loop(0, rec_ref.shape[1], note, jnp.int32(0), unroll=8)


def list_sources(src_ref):
    lane = lane_ids()
    row = lax.broadcasted_iota(jnp.int32, (8, LANES), 0)
    start = corner()
    points = []
    for s in range(src_ref.shape[0]):
        h = src_ref[s, 0] - start[0]
        w = src_ref[s, 1] - start[1]
        d = src_ref[s, 2] - start[2] + HALO
        near = (h >= 0) & (h < TALL) & (w >= 0) & (w < BROAD) & (d >= 0) & (d < DEEP + 2 * HALO)
        h = jnp.clip(h, 0, TALL - 1)
        w = jnp.clip(w, 0, BROAD - 1)
        d = jnp.clip(d, 0, DEEP + 2 * HALO - 1)
        place = (d // 2 + LANES - HALO // 2) % LANES
        points.append((near, d % 2, h, w % COLS, (row == w // COLS) & (lane == place)))
    return points


def sweep(now, old, p_ref, first, trips, layers):
    def chunk(i, carry):
        for u in range(layers):
            h = first(i) + u
            for part in range(2):
                js = range(part * COLS // 2, (part + 1) * COLS // 2)
                for parity in range(2):
                    side = {j: now[1 - parity, h, j] for j in js}
                    rolled = {j: pltpu.roll(side[j], 127 if parity else 1, 1) for j in js}
                    near = range(max(js[0] - 1, 0), min(js[-1] + 2, COLS))
                    mine = {j: now[parity, h, j] for j in near}
                    if part == 0:
                        mine[-1] = pltpu.roll(now[parity, h, COLS - 1], 1, 0)
                    else:
                        mine[COLS] = pltpu.roll(now[parity, h, 0], 7, 0)
                    known = {}
                    for j in js:
                        past = old[parity, h, j]
                        total = now[parity, h - 1, j] + now[parity, h + 1, j]
                        total = total + (mine[j - 1] + mine[j + 1]) + side[j]
                        known[j] = (past, total - 6.0 * past)
                    for j in js:
                        past, total = known[j]
                        old[parity, h, j] = past + p_ref[parity, h, j] * (total + rolled[j])
        return carry

    lax.fori_loop(0, trips, chunk, 0)


def inject(field, points, sig_ref, t, base, inside):
    some = points[0][0]
    for point in points[1:]:
        some = some | point[0]

    @pl.when(some)
    def _():
        for s, (near, parity, h, j, spot) in enumerate(points):

            @pl.when(near & inside(h))
            def _():
                add = jnp.where(spot, sig_ref[s, t], jnp.float32(0.0))
                field[parity, h - base, j] = field[parity, h - base, j] + add


def keep(field, todo, hist, t, base):
    def one(i, carry):
        row = field[todo[4, i], todo[1, i] - base, todo[2, i], pl.ds(todo[3, i], 1), :]
        hist[i, pl.ds(t, 1), :] = row
        return carry

    lax.fori_loop(0, todo[6, 0], one, 0)


def gather(trace, todo, hist, early):
    lane = lax.broadcasted_iota(jnp.int32, (STEPS, LANES), 1)
    step = lax.broadcasted_iota(jnp.int32, (STEPS, LANES), 0)

    def one(i, carry):
        number, h = todo[0, i], todo[1, i]
        moved = pltpu.roll(hist[i], (number - todo[5, i] + LANES) % LANES, 1)
        done_early = (h > HALO + step) & (h < TALL - HALO - 1 - step)
        now = done_early if early else ~done_early
        trace[...] = jnp.where((lane == number) & now, moved, trace[...])
        return carry

    lax.fori_loop(0, todo[6, 0], one, 0)


def inner_kernel(src_ref, sig_ref, todo, *refs):
    a_ref, b_ref, p_ref, trace_ref, temp, hist = refs[4:]
    fill_own((a_ref, b_ref, p_ref), temp, *refs[:4])
    points = list_sources(src_ref)

    def step(now, old, t):
        sweep(now, old, p_ref, lambda i: t + 1 + 2 * i, HALF - 1 - t, 2)
        inject(old, points, sig_ref, t, HALO, lambda h: (h > HALO + t) & (h < HALO + HIGH - 1 - t))
        keep(old, todo, hist, t, HALO)

    def pair(i, carry):
        step(a_ref, b_ref, 2 * i)
        step(b_ref, a_ref, 2 * i + 1)
        return carry

    lax.fori_loop(0, HALF // 2, pair, 0)
    trace_ref[...] = jnp.zeros((STEPS, LANES), jnp.float32)
    gather(trace_ref, todo, hist, True)


def march_kernel(src_ref, sig_ref, todo, *refs):
    own = refs[:3]
    early_ref, mains, under_edge, over_edge = refs[3], refs[4:7], refs[7], refs[8]
    out_ref, trace_ref = refs[9:11]
    a_ref, b_ref, p_ref, temp, hist = refs[11:]
    fields = (a_ref, b_ref, p_ref)

    def take(h, carry):
        for ref, got in zip(fields, own):
            for parity in range(2):
                ref[parity, HALO + h] = got[parity, h]
        return carry

    lax.fori_loop(0, HIGH, take, 0, unroll=2)
    fill_edges(fields, mains, temp, under_edge, lambda i: (HALO - 1 - i, i), 0)
    fill_edges(fields, mains, temp, over_edge, lambda i: (HALO + i, 2 * HALO - 1 - i), HIGH)
    points = list_sources(src_ref)

    def step(now, old, t):
        early = t < HALF - 1
        full = TALL - 2 * (t + 1)
        gap = jnp.where(early, HIGH - 2 * (t + 1), 0)
        eights = jnp.where(early, HIGH // 4, full // 8)
        rest = jnp.where(early, 0, full % 8)
        sweep(
            now,
            old,
            p_ref,
            lambda i: t + 1 + 8 * i + jnp.where(i >= HIGH // 8, gap, 0),
            eights,
            8,
        )
        sweep(now, old, p_ref, lambda i: t + 1 + 8 * eights, rest // 4, 4)
        sweep(now, old, p_ref, lambda i: t + 1 + full - 2, (rest % 4) // 2, 2)
        inject(old, points, sig_ref, t, 0, lambda h: (h <= HALO + t) | (h >= HALO + HIGH - 1 - t))
        keep(old, todo, hist, t, 0)

    def pair(i, carry):
        step(a_ref, b_ref, 2 * i)
        step(b_ref, a_ref, 2 * i + 1)
        return carry

    lax.fori_loop(0, STEPS // 2, pair, 0)

    trace_ref[0] = early_ref[...]
    gather(trace_ref.at[0], todo, hist, False)
    for i in range(1, trace_ref.shape[0]):
        trace_ref[i] = trace_ref[0]

    lane = lane_ids()
    plain = temp.at[0]

    def hand_on(h, carry):
        for j in range(COLS):
            even, odd = a_ref[0, HALO + h, j], a_ref[1, HALO + h, j]
            joined = jnp.where(lane < 64, even, pltpu.roll(odd, 64, 1))
            plain[pl.ds(j, 8, stride=COLS), :] = joined
        out_ref[h] = plain[pl.ds(HALO, WIDE), :]
        return carry

    lax.fori_loop(0, HIGH, hand_on, 0, unroll=4)


def order_kernel(split_ref, out_ref):
    order = in_order()

    def layer(h, carry):
        for j in range(WIDE // 8):
            rows = pl.ds(8 * j, 8)
            out_ref[h, rows, :] = regroup(split_ref[h, rows, :], order)
        return carry

    lax.fori_loop(0, split_ref.shape[0], layer, 0)


def relay_kernel(got_ref, out_ref):
    total = got_ref[0]
    for i in range(1, got_ref.shape[0]):
        total = total + got_ref[i]
    for i in range(out_ref.shape[0]):
        out_ref[i] = total


def total_kernel(got_ref, out_ref):
    total = got_ref[0]
    for i in range(1, got_ref.shape[0]):
        total = total + got_ref[i]
    out_ref[...] = total


def field(*shape):
    return jax.ShapeDtypeStruct(shape, jnp.float32)


def call(kernel, name, outs, ins, scratch=(), scalars=0, limit=8, listed=False):
    out_shape = [field(*shape) for shape in outs]
    out_specs = [VMEM for _ in outs]
    if listed:
        out_shape.append(jax.ShapeDtypeStruct((8, LANES), jnp.int32))
        out_specs.append(SMEM)
    return pl.pallas_call(
        kernel,
        out_shape=tuple(out_shape),
        in_specs=[SMEM] * scalars + [VMEM] * (len(ins) - scalars),
        out_specs=tuple(out_specs),
        scratch_shapes=list(scratch),
        name=name,
        compiler_params=pltpu.CompilerParams(vmem_limit_bytes=limit << 20),
    )(*ins)


def shift(x, axis, move):
    size = lax.axis_size(axis)
    pairs = [(i, i + move) for i in range(size) if 0 <= i + move < size]
    return lax.ppermute(x, axis, pairs)


def per_device(
    pressure_now, pressure_old, classes, admittance, source_cells, source_signal, receiver_cells
):
    face = (HIGH, 3, HALO, LANES)
    block = (HIGH, WIDE, DEEP)
    s, head, tail = pl.pallas_call(
        pack_kernel,
        out_shape=(field(HIGH, 3, WIDE, LANES), field(*face), field(*face)),
        in_specs=[HBM] * 4,
        out_specs=(HBM,) * 3,
        scratch_shapes=[
            pltpu.SMEM(admittance.shape, jnp.float32),
            pltpu.VMEM(block, jnp.float32),
            pltpu.VMEM(block, jnp.float32),
            pltpu.VMEM(block, jnp.int32),
            pltpu.VMEM((HIGH, 3, WIDE, LANES), jnp.float32),
            pltpu.VMEM(face, jnp.float32),
            pltpu.VMEM(face, jnp.float32),
            pltpu.SemaphoreType.DMA((PARTS, 3)),
            pltpu.SemaphoreType.DMA((PARTS, 3)),
            pltpu.SemaphoreType.DMA,
        ],
        name="pack",
        compiler_params=pltpu.CompilerParams(vmem_limit_bytes=PACK_LIMIT),
    )(admittance, pressure_now, pressure_old, classes)
    over, under = shift(s, "hgt", -1), shift(s, "hgt", 1)
    before, after = shift(tail, "wid", 1), shift(head, "wid", -1)
    strip = (HIGH, (BROAD - HALO) // 2, LANES)
    mine, todo = call(
        own_strip_kernel,
        "own_strip",
        [(HIGH, WIDE, LANES)],
        [receiver_cells.T, s],
        scalars=1,
        listed=True,
    )
    before, after, mine = lax.optimization_barrier((before, after, mine))
    to_left, to_right = call(strip_kernel, "strip", [strip, strip], [mine, before, after])
    from_right = shift(to_left, "len", -1)
    from_left = shift(to_right, "len", 1)
    wide_rim, long_rim = (HALF, 3 * 2 * HALO, LANES), (HALF, BROAD, LANES)
    low, top = call(wide_rim_kernel, "wide_rim", [wide_rim, wide_rim], [before, after])
    over_rim, under_rim = shift(low, "hgt", -1), shift(top, "hgt", 1)
    edge, low, top = call(
        long_rim_kernel,
        "long_rim",
        [(HIGH, BROAD, LANES), long_rim, long_rim],
        [from_right, from_left],
    )
    under_edge = shift(top, "hgt", 1)
    low, under = lax.optimization_barrier((low, under))
    over_edge = shift(low, "hgt", -1)
    own = (2, HIGH, COLS, 8, LANES)
    temp = pltpu.VMEM((4, BROAD, LANES), jnp.float32)
    hist = pltpu.VMEM((LANES, STEPS, LANES), jnp.float32)
    now, old, gain, early = call(
        inner_kernel,
        "inner",
        [own, own, own, (STEPS, LANES)],
        [source_cells, source_signal.T, todo]
        + [s, edge, before, after],
        scratch=[temp, hist],
        scalars=3,
        limit=8,
    )
    halos = (2, 2 * HALO, COLS, 8, LANES)
    mains = call(
        beside_kernel,
        "beside",
        [halos] * 3,
        [under, under_rim, over, over_rim],
        scratch=[temp],
        limit=16,
    )
    state = pltpu.VMEM((2, TALL, COLS, 8, LANES), jnp.float32)
    depth = lax.axis_size("len")
    sides = lax.axis_size("wid") * lax.axis_size("hgt")
    split, traces = call(
        march_kernel,
        "march",
        [(HIGH, WIDE, LANES), (depth, STEPS, LANES)],
        [source_cells, source_signal.T, todo, now, old, gain, early]
        + [*mains, under_edge, over_edge],
        scratch=[state, state, state, temp, hist],
        scalars=3,
        limit=20,
    )
    traces = lax.all_to_all(traces, "len", 0, 0, tiled=True)
    (traces,) = call(relay_kernel, "relay", [(sides, STEPS, LANES)], [traces])
    traces = lax.all_to_all(traces, ("wid", "hgt"), 0, 0, tiled=True)
    (now,) = call(order_kernel, "order", [(HIGH, WIDE, DEEP)], [split])
    (traces,) = call(total_kernel, "total", [(STEPS, LANES)], [traces])
    return now, traces


def solution(mesh):
    block = P("hgt", "wid", "len")
    return jax.shard_map(
        per_device,
        mesh=mesh,
        in_specs=(block, block, block, P(), P(), P(), P()),
        out_specs=(block, P()),
        check_vma=False,
    )
```
